32 devices in a mesh: gx: 8 (over z, core), gy: 4 (over y, x).
Axes of the slice: x: 2, y: 2, z: 4, core: 2. Of those that a mesh axis runs over, the one named last changes fastest.
Arguments:
- field: float32 [256, 128, 256], P('gx', 'gy'), may hold values from -192 to 192
- cond_x: float32 [256, 128, 256], P('gx', 'gy'), may hold values from 1 to 4
- cond_y: float32 [256, 128, 256], P('gx', 'gy'), may hold values from 1 to 4
- cross_weight: float32 [256, 128, 256], P('gx', 'gy'), may hold values from -4 to 4
Outputs:
- field_next: float32 [256, 128, 256], P('gx', 'gy')
The draws below stay inside these ranges and needn't reach their ends.
All inputs are finite; a program needn't handle non-finite values.
Results may differ from the reference program's by a relative error of at most 0.0007.
Values sent between devices are 32-bit elements; how exact they have to be, the bound alone decides.
A program may use at most 64 MiB of HBM per device.

```python
import math
import jax
import jax.numpy as jnp
from jax import lax

NZ = 256
NX = 256
NY = 128


def draw_field(key, part):
    values = 32.0 * jax.random.normal(key, (NX, NY, NZ), jnp.float32)
    return jnp.clip(values, -192.0, 192.0)


def block_scale(rng, extent, cuts, low, high):
    loudness = 1.0
    for axis_at, shards_of in cuts:
        draws = jax.random.uniform(jax.random.fold_in(jax.random.fold_in(rng, 6), axis_at), (shards_of,), jnp.float32, low / len(cuts), high / len(cuts))
        loudness = loudness * jnp.repeat(jnp.exp(draws), extent[axis_at] // shards_of).reshape((-1,) + (1,) * (len(extent) - 1 - axis_at))
    return loudness


def setup_inputs(seed: int = 0) -> dict:
    keys = jax.random.split(jax.random.key(seed), 5)
    return {
        "field": draw_field(jax.random.fold_in(keys[4], 71), 0),
        "cond_x": jnp.clip(jnp.exp(math.log(4.0) - 1.3862944 * jax.random.uniform(keys[1], (NX, NY, NZ), jnp.float32) ** block_scale(keys[1], (NX, NY, NZ), ((0, 8), (1, 4)), -0.2, 0.2)), 1.0, 4.0),
        "cond_y": jnp.clip(jnp.exp(math.log(4.0) - 1.3862944 * jax.random.uniform(keys[2], (NX, NY, NZ), jnp.float32) ** block_scale(keys[2], (NX, NY, NZ), ((0, 8), (1, 4)), -0.2, 0.2)), 1.0, 4.0),
        "cross_weight": jnp.clip(jax.random.uniform(keys[3], (NX, NY, NZ), jnp.float32, -4.0, 4.0) * block_scale(keys[3], (NX, NY, NZ), ((0, 8), (1, 4)), -0.4, 0.0), -4.0, 4.0),
    }


step_dt = 16384.0


def thomas(lower_band, center, upper_band, right_side):
    def forward(carry, items):
        prev_ratio, prev_value = carry
        below_term, middle, above_term, right_term = items
        denominator = middle - below_term * prev_ratio
        next_ratio = above_term / denominator
        next_value = (right_term - below_term * prev_value) / denominator
        return (next_ratio, next_value), (next_ratio, next_value)

    start = (jnp.zeros_like(center[0]), jnp.zeros_like(right_side[0]))
    leftover, (ratios, values) = lax.scan(forward, start, (lower_band, center, upper_band, right_side))

    def backward(after, items):
        ratio, value = items
        here = value - ratio * after
        return here, here

    remaining, result = lax.scan(backward, jnp.zeros_like(right_side[0]), (ratios, values), reverse=True)
    return result


def line_solve(coef, right_side):
    following = jnp.concatenate([coef[1:], jnp.zeros_like(coef[:1])], axis=0)
    lower_band = -step_dt * coef
    upper_band = -step_dt * following
    center = 1.0 + step_dt * (coef + following)
    return thomas(lower_band, center, upper_band, right_side)


def reference(field, cond_x, cond_y, cross_weight):
    padded = jnp.pad(field, ((1, 1), (1, 1), (0, 0)))
    mixed = padded[2:, 2:] - padded[2:, :-2] - padded[:-2, 2:] + padded[:-2, :-2]
    source = field + cross_weight * mixed * 0.25
    half = line_solve(cond_x, source)
    turned = line_solve(jnp.moveaxis(cond_y, 1, 0), jnp.moveaxis(half, 1, 0))
    return jnp.moveaxis(turned, 1, 0)
```

```python
import functools
import jax
import jax.numpy as jnp
from jax import lax
from jax.sharding import PartitionSpec as P
from jax.experimental import pallas as pl
from jax.experimental.pallas import tpu as pltpu

step_dt = 16384.0
LANES = 128
ROWS = 8
MESH = pl.DeviceIdType.MESH


def split_tiles(tiles, count):
    per_owner = next(p for p in range(1, tiles + 1) if tiles % p == 0 and p * count >= tiles)
    return per_owner, tiles // per_owner


class Sweep:
    def __init__(self, axis, count, tiles, refs):
        self.axis, self.count, self.tiles = axis, count, tiles
        self.per, self.owners = split_tiles(tiles, count)
        (self.t, self.rt, self.b, self.rb, self.s, self.rs, self.pe, self.sems) = refs
        self.me = lax.axis_index(axis)

    def others(self):
        return [lax.rem(self.me + d, self.count) for d in range(1, self.count)]

    def own(self):
        return pl.ds(self.me * self.per, self.per)

    def guarded(self, index, body):
        if self.owners == self.count:
            body()
        else:
            pl.when(index < self.owners)(body)

    def copy(self, kind, src, dst, target, sender):
        return pltpu.make_async_remote_copy(
            src_ref=src,
            dst_ref=dst,
            send_sem=self.sems.at[2 * kind, target],
            recv_sem=self.sems.at[2 * kind + 1, sender],
            device_id={self.axis: target},
            device_id_type=MESH,
        )

    def up(self, kind, target):
        mine, there = ((self.t, self.rt), (self.b, self.rb))[kind]
        return self.copy(kind, mine.at[pl.ds(target * self.per, self.per)], there.at[self.me], target, self.me)

    def up_from(self, kind, sender):
        mine, there = ((self.t, self.rt), (self.b, self.rb))[kind]
        return self.copy(kind, mine.at[pl.ds(0, self.per)], there.at[sender], sender, sender)

    def send(self, kind):
        for target in self.others():
            self.guarded(target, lambda target=target: self.up(kind, target).start())

        def keep():
            mine, there = ((self.t, self.rt), (self.b, self.rb))[kind]
            there[self.me] = mine[self.own()]

        self.guarded(self.me, keep)

    def prepare(self):
        def body():
            for sender in self.others():
                self.up_from(0, sender).wait_recv()
            shape = (self.per, ROWS, LANES)
            resistance = jnp.zeros(shape, jnp.float32)
            for j in range(self.count):
                inverse = 1.0 / (self.rt[j, :, 2] * resistance + self.rt[j, :, 3])
                self.pe[j, :, 0] = resistance
                self.pe[j, :, 1] = inverse
                resistance = (self.rt[j, :, 0] * resistance + self.rt[j, :, 1]) * inverse
            self.pe[self.count, :, 0] = resistance

        self.guarded(self.me, body)

    def back(self, target):
        return self.copy(2, self.s.at[target], self.rs.at[self.own()], target, self.me)

    def back_from(self, owner):
        return self.copy(2, self.s.at[owner], self.rs.at[pl.ds(owner * self.per, self.per)], owner, owner)

    def solve(self):
        def body():
            for sender in self.others():
                self.up_from(1, sender).wait_recv()
            shape = (self.per, ROWS, LANES)
            offset = jnp.zeros(shape, jnp.float32)
            offsets = []
            for j in range(self.count):
                offsets.append(offset)
                offset = offset * self.pe[j, :, 1] + self.rb[j, :, 0] - self.pe[j + 1, :, 0] * self.rb[j, :, 1]
            flux = jnp.zeros(shape, jnp.float32)
            for j in reversed(range(self.count)):
                flux = (flux - self.rt[j, :, 2] * offsets[j] - self.rb[j, :, 1]) * self.pe[j, :, 1]
                self.s[j, :, 0] = self.pe[j, :, 0] * flux + offsets[j]
                self.s[j, :, 1] = flux
            for target in self.others():
                self.back(target).start()
            self.rs[self.own()] = self.s[self.me]

        self.guarded(self.me, body)

    def receive(self):
        for d in range(1, self.count):
            owner = lax.rem(self.me + d, self.count)
            self.guarded(owner, lambda owner=owner: self.back_from(owner).wait_recv())

    def drain(self):
        def returned():
            for target in self.others():
                self.back(target).wait_send()

        for target in self.others():
            for kind in (0, 1):
                self.guarded(target, lambda target=target, kind=kind: self.up(kind, target).wait_send())
        self.guarded(self.me, returned)


def kernel(nx, ny, lx, ly, nh, *refs):
    field, cond_x, cond_y, weight, out = refs[:5]
    F, KX, KY, R, RY, HALF, HT, O, xh, ys, yh, ch, dl = refs[5:18]
    in_sem, out_sem, halo_send, halo_recv = refs[18:22]
    x_refs, y_refs = refs[22:30], refs[30:38]
    rtx, rty = ly // ROWS, lx // ROWS
    mx, my = lax.axis_index("gx"), lax.axis_index("gy")
    X = Sweep("gx", nx, nh * rtx, x_refs)
    Y = Sweep("gy", ny, nh * rty, y_refs)

    around = [(-1, 0), (1, 0), (0, -1), (0, 1), (-1, -1), (-1, 1), (1, -1), (1, 1)]

    def exists(dx, dy):
        there = None
        for d, m, n in ((dx, mx, nx), (dy, my, ny)):
            if d:
                ok = (m > 0) if d < 0 else (m < n - 1)
                there = ok if there is None else jnp.logical_and(there, ok)
        return there

    barrier = pltpu.get_barrier_semaphore()
    for target in X.others():
        pl.semaphore_signal(barrier, inc=1, device_id={"gx": target}, device_id_type=MESH)
    for target in Y.others():
        pl.semaphore_signal(barrier, inc=1, device_id={"gy": target}, device_id_type=MESH)
    for dx, dy in around[4:]:
        @pl.when(exists(dx, dy))
        def _(dx=dx, dy=dy):
            pl.semaphore_signal(barrier, inc=1, device_id={"gx": mx + dx, "gy": my + dy}, device_id_type=MESH)

    def lanes(h):
        return pl.ds(h * LANES, LANES)

    def load(k, h):
        src, dst = (
            (field, F.at[h, pl.ds(ly, lx * ly)]), (cond_x, KX.at[h]), (cond_y, KY.at[h]), (weight, R.at[h])
        )[k]
        return pltpu.make_async_copy(src.at[:, lanes(h)], dst, in_sem.at[k, h])

    for k in range(4):
        for h in range(nh):
            load(k, h).start()

    for h in range(nh):
        load(0, h).wait()
    for h in range(nh):
        ys[0, h] = F[h, pl.ds(ly, lx, stride=ly), :]
        ys[1, h] = F[h, pl.ds(ly + ly - 1, lx, stride=ly), :]

    def halo(k):
        dx, dy = around[k]
        if dy == 0:
            src = F.at[:, pl.ds(ly if dx < 0 else lx * ly, ly), :]
            dst = xh.at[1 if dx < 0 else 0]
        elif dx == 0:
            src = ys.at[0 if dy < 0 else 1]
            dst = yh.at[1 if dy < 0 else 0]
        else:
            src = ys.at[0 if dy < 0 else 1, :, pl.ds(0 if dx < 0 else lx - ROWS, ROWS), :]
            dst = ch.at[2 * (1 if dy < 0 else 0) + (1 if dx < 0 else 0)]
        return pltpu.make_async_remote_copy(
            src_ref=src,
            dst_ref=dst,
            send_sem=halo_send.at[k],
            recv_sem=halo_recv.at[around.index((-dx, -dy))],
            device_id={"gx": mx + dx, "gy": my + dy},
            device_id_type=MESH,
        )

    def halo_in(k):
        dx, dy = around[k]
        if dy == 0:
            dst = xh.at[0 if dx < 0 else 1]
        elif dx == 0:
            dst = yh.at[0 if dy < 0 else 1]
        else:
            dst = ch.at[2 * (0 if dy < 0 else 1) + (0 if dx < 0 else 1)]
        return dst, lambda: pltpu.make_async_remote_copy(
            src_ref=dst,
            dst_ref=dst,
            send_sem=halo_send.at[k],
            recv_sem=halo_recv.at[k],
            device_id={"gx": mx + dx, "gy": my + dy},
            device_id_type=MESH,
        )

    diagonal = sum(jnp.where(exists(dx, dy), 1, 0) for dx, dy in around[4:])
    pl.semaphore_wait(barrier, nx - 1 + ny - 1 + diagonal)

    for k, (dx, dy) in enumerate(around):
        @pl.when(exists(dx, dy))
        def _(k=k):
            halo(k).start()

    def rows(i, n):
        return pl.ds(pl.multiple_of(i * n, n), n)

    def put_tiles(ref, h, per_plane, values):
        for c, value in enumerate(values):
            for t in range(per_plane):
                ref[h * per_plane + t, c] = value[t * ROWS:(t + 1) * ROWS]

    def get_tiles(ref, h, per_plane, c):
        return jnp.concatenate([ref[h * per_plane + t, c] for t in range(per_plane)], axis=0)

    for k in (1,):
        for h in range(nh):
            load(k, h).wait()

    def transfer(length, width, resistance_at):
        def steps(g, carry):
            x0, j0, x1, j1 = carry
            for r in range(ROWS):
                rho = resistance_at(g * ROWS + r)
                x0 = x0 + rho * j0
                x1 = x1 + rho * j1
                j0 = j0 + x0
                j1 = j1 + x1
            return x0, j0, x1, j1

        zero = jnp.zeros((width, LANES), jnp.float32)
        one = jnp.ones((width, LANES), jnp.float32)
        x0, j0, x1, j1 = lax.fori_loop(0, length // ROWS, steps, (one, zero, zero, one))
        return x0, x1, j0, j1

    for h in range(nh):
        def resistance_x(i, h=h):
            rho = (1.0 / step_dt) / KX[h, rows(i, ly), :]
            KX[h, rows(i, ly), :] = rho
            return rho

        put_tiles(X.t, h, rtx, transfer(lx, ly, resistance_x))
    X.send(0)

    for h in range(nh):
        load(3, h).wait()
    for k, (dx, dy) in enumerate(around):
        @pl.when(exists(dx, dy))
        def _(k=k):
            halo_in(k)[1]().wait_recv()

        @pl.when(jnp.logical_not(exists(dx, dy)))
        def _(k=k):
            dst = halo_in(k)[0]
            dst[...] = jnp.zeros(dst.shape, jnp.float32)

    for h in range(nh):
        F[h, pl.ds(0, ly), :] = xh[0, h]
        F[h, pl.ds((lx + 1) * ly, ly), :] = xh[1, h]
        for side in range(2):
            edge = yh[side, h]
            before = jnp.concatenate([ch[2 * side, h, ROWS - 1:, :], edge[:-1]], axis=0)
            after = jnp.concatenate([edge[1:], ch[2 * side + 1, h, :1, :]], axis=0)
            dl[side, h] = after - before

    row = lax.broadcasted_iota(jnp.int32, (ly, LANES), 0)
    for h in range(nh):
        def steps(g, carry, h=h):
            x, j = carry
            low = dl[0, h, rows(g, ROWS), :]
            high = dl[1, h, rows(g, ROWS), :]
            for r in range(ROWS):
                i = g * ROWS + r
                across = F[h, rows(i + 2, ly), :] - F[h, rows(i, ly), :]
                above = jnp.where(row == ly - 1, high[r:r + 1], pltpu.roll(across, ly - 1, 0))
                below = jnp.where(row == 0, low[r:r + 1], pltpu.roll(across, 1, 0))
                source = F[h, rows(i + 1, ly), :] + R[h, rows(i, ly), :] * (above - below) * 0.25
                R[h, rows(i, ly), :] = source
                x = x + KX[h, rows(i, ly), :] * j
                j = j + (x - source)
            return x, j

        zero = jnp.zeros((ly, LANES), jnp.float32)
        put_tiles(X.b, h, rtx, lax.fori_loop(0, lx // ROWS, steps, (zero, zero)))
    X.send(1)

    for h in range(nh):
        load(2, h).wait()
    for h in range(nh):
        def resistance_y(i, h=h):
            rho = (1.0 / step_dt) / KY[h, pl.ds(i, lx, stride=ly), :]
            RY[h, rows(i, lx), :] = rho
            return rho

        put_tiles(Y.t, h, rty, transfer(ly, lx, resistance_y))
    Y.send(0)

    X.prepare()
    X.solve()
    Y.prepare()
    X.receive()

    for h in range(nh):
        def steps(g, carry, h=h):
            x, j = carry
            for r in range(ROWS):
                i = g * ROWS + r
                x = x + KX[h, rows(i, ly), :] * j
                j = j + (x - R[h, rows(i, ly), :])
                HALF[h, rows(i, ly), :] = x
            return x, j

        start = (get_tiles(X.rs, h, rtx, 0), get_tiles(X.rs, h, rtx, 1))
        lax.fori_loop(0, lx // ROWS, steps, start)

        def steps_y(g, carry, h=h):
            x, j = carry
            for r in range(ROWS):
                i = g * ROWS + r
                half = HALF[h, pl.ds(i, lx, stride=ly), :]
                HT[h, rows(i, lx), :] = half
                x = x + RY[h, rows(i, lx), :] * j
                j = j + (x - half)
            return x, j

        zero = jnp.zeros((lx, LANES), jnp.float32)
        put_tiles(Y.b, h, rty, lax.fori_loop(0, ly // ROWS, steps_y, (zero, zero)))
    Y.send(1)
    Y.solve()
    Y.receive()

    def store(h):
        return pltpu.make_async_copy(O.at[h], out.at[:, lanes(h)], out_sem.at[h])

    for h in range(nh):
        def steps(g, carry, h=h):
            x, j = carry
            for r in range(ROWS):
                i = g * ROWS + r
                x = x + RY[h, rows(i, lx), :] * j
                j = j + (x - HT[h, rows(i, lx), :])
                O[h, pl.ds(i, lx, stride=ly), :] = x
            return x, j

        start = (get_tiles(Y.rs, h, rty, 0), get_tiles(Y.rs, h, rty, 1))
        lax.fori_loop(0, ly // ROWS, steps, start)
        store(h).start()

    for k, (dx, dy) in enumerate(around):
        @pl.when(exists(dx, dy))
        def _(k=k):
            halo(k).wait_send()
    X.drain()
    Y.drain()
    for h in range(nh):
        store(h).wait()


def sweep_scratch(count, tiles):
    per, owners = split_tiles(tiles, count)
    return [
        pltpu.VMEM((tiles, 4, ROWS, LANES), jnp.float32),
        pltpu.VMEM((count, per, 4, ROWS, LANES), jnp.float32),
        pltpu.VMEM((tiles, 2, ROWS, LANES), jnp.float32),
        pltpu.VMEM((count, per, 2, ROWS, LANES), jnp.float32),
        pltpu.VMEM((count, per, 2, ROWS, LANES), jnp.float32),
        pltpu.VMEM((tiles, 2, ROWS, LANES), jnp.float32),
        pltpu.VMEM((count + 1, per, 2, ROWS, LANES), jnp.float32),
        pltpu.SemaphoreType.DMA((6, count)),
    ]


def shards(nx, ny, field, cond_x, cond_y, cross_weight):
    lx, ly, nz = field.shape
    nh = nz // LANES
    cells = (nh, lx * ly, LANES)
    flat = [a.reshape(lx * ly, nz) for a in (field, cond_x, cond_y, cross_weight)]
    scratch = [
        pltpu.VMEM((nh, (lx + 2) * ly, LANES), jnp.float32),
        *[pltpu.VMEM(cells, jnp.float32)] * 7,
        pltpu.VMEM((2, nh, ly, LANES), jnp.float32),
        pltpu.VMEM((2, nh, lx, LANES), jnp.float32),
        pltpu.VMEM((2, nh, lx, LANES), jnp.float32),
        pltpu.VMEM((4, nh, ROWS, LANES), jnp.float32),
        pltpu.VMEM((2, nh, lx, LANES), jnp.float32),
        pltpu.SemaphoreType.DMA((4, nh)),
        pltpu.SemaphoreType.DMA((nh,)),
        pltpu.SemaphoreType.DMA((8,)),
        pltpu.SemaphoreType.DMA((8,)),
        *sweep_scratch(nx, nh * ly // ROWS),
        *sweep_scratch(ny, nh * lx // ROWS),
    ]
    result = pl.pallas_call(
        functools.partial(kernel, nx, ny, lx, ly, nh),
        out_shape=jax.ShapeDtypeStruct((lx * ly, nz), jnp.float32),
        in_specs=[pl.BlockSpec(memory_space=pl.ANY)] * 4,
        out_specs=pl.BlockSpec(memory_space=pl.ANY),
        scratch_shapes=scratch,
        compiler_params=pltpu.CompilerParams(
            collective_id=0, has_side_effects=True, vmem_limit_bytes=40 * 1024 * 1024
        ),
        cost_estimate=pl.CostEstimate(
            flops=60 * lx * ly * nz, bytes_accessed=20 * lx * ly * nz, transcendentals=0
        ),
        name="adi_step",
    )(*flat)
    return result.reshape(lx, ly, nz)


def solution(mesh):
    spec = P("gx", "gy", None)
    return jax.shard_map(
        functools.partial(shards, mesh.shape["gx"], mesh.shape["gy"]),
        mesh=mesh,
        in_specs=(spec,) * 4,
        out_specs=spec,
        check_vma=False,
    )
```

```python
import functools
import jax
import jax.numpy as jnp
from jax import lax
from jax.sharding import PartitionSpec as P
from jax.experimental import pallas as pl
from jax.experimental.pallas import tpu as pltpu

step_dt = 16384.0
LANES = 128
ROWS = 8
MESH = pl.DeviceIdType.MESH


def split_tiles(tiles, count):
    per_owner = next(p for p in range(1, tiles + 1) if tiles % p == 0 and p * count >= tiles)
    return per_owner, tiles // per_owner


class Sweep:
    def __init__(self, axis, count, tiles, refs):
        self.axis, self.count, self.tiles = axis, count, tiles
        self.per, self.owners = split_tiles(tiles, count)
        (self.t, self.rt, self.b, self.rb, self.s, self.rs, self.pe, self.sems) = refs
        self.me = lax.axis_index(axis)

    def others(self):
        return [lax.rem(self.me + d, self.count) for d in range(1, self.count)]

    def own(self):
        return pl.ds(self.me * self.per, self.per)

    def guarded(self, index, body):
        if self.owners == self.count:
            body()
        else:
            pl.when(index < self.owners)(body)

    def copy(self, kind, src, dst, target, sender):
        return pltpu.make_async_remote_copy(
            src_ref=src,
            dst_ref=dst,
            send_sem=self.sems.at[2 * kind, target],
            recv_sem=self.sems.at[2 * kind + 1, sender],
            device_id={self.axis: target},
            device_id_type=MESH,
        )

    def up(self, kind, target):
        mine, there = ((self.t, self.rt), (self.b, self.rb))[kind]
        return self.copy(kind, mine.at[pl.ds(target * self.per, self.per)], there.at[self.me], target, self.me)

    def up_from(self, kind, sender):
        mine, there = ((self.t, self.rt), (self.b, self.rb))[kind]
        return self.copy(kind, mine.at[pl.ds(0, self.per)], there.at[sender], sender, sender)

    def send(self, kind, part=0, parts=1):
        low, high = self.owners * part // parts, self.owners * (part + 1) // parts

        def inside(index, body):
            if parts == 1:
                self.guarded(index, body)
            else:
                pl.when(jnp.logical_and(index >= low, index < high))(body)

        def keep():
            mine, there = ((self.t, self.rt), (self.b, self.rb))[kind]
            there[self.me] = mine[self.own()]

        for target in self.others():
            inside(target, lambda target=target: self.up(kind, target).start())
        inside(self.me, keep)

    def prepare(self):
        def body():
            for sender in self.others():
                self.up_from(0, sender).wait_recv()
            shape = (self.per, ROWS, LANES)
            resistance = jnp.zeros(shape, jnp.float32)
            for j in range(self.count):
                inverse = 1.0 / (self.rt[j, :, 2] * resistance + self.rt[j, :, 3])
                self.pe[j, :, 0] = resistance
                self.pe[j, :, 1] = inverse
                resistance = (self.rt[j, :, 0] * resistance + self.rt[j, :, 1]) * inverse
            self.pe[self.count, :, 0] = resistance

        self.guarded(self.me, body)

    def back(self, target):
        return self.copy(2, self.s.at[target], self.rs.at[self.own()], target, self.me)

    def back_from(self, owner):
        return self.copy(2, self.s.at[owner], self.rs.at[pl.ds(owner * self.per, self.per)], owner, owner)

    def solve(self):
        def body():
            for sender in self.others():
                self.up_from(1, sender).wait_recv()
            shape = (self.per, ROWS, LANES)
            offset = jnp.zeros(shape, jnp.float32)
            offsets = []
            for j in range(self.count):
                offsets.append(offset)
                offset = offset * self.pe[j, :, 1] + self.rb[j, :, 0] - self.pe[j + 1, :, 0] * self.rb[j, :, 1]
            flux = jnp.zeros(shape, jnp.float32)
            for j in reversed(range(self.count)):
                flux = (flux - self.rt[j, :, 2] * offsets[j] - self.rb[j, :, 1]) * self.pe[j, :, 1]
                self.s[j, :, 0] = self.pe[j, :, 0] * flux + offsets[j]
                self.s[j, :, 1] = flux
            for target in self.others():
                self.back(target).start()
            self.rs[self.own()] = self.s[self.me]

        self.guarded(self.me, body)

    def receive(self, part, parts):
        low, high = self.owners * part // parts, self.owners * (part + 1) // parts
        for owner in range(low, high):
            pl.when(self.me != owner)(lambda owner=owner: self.back_from(owner).wait_recv())

    def drain(self):
        def returned():
            for target in self.others():
                self.back(target).wait_send()

        for target in self.others():
            for kind in (0, 1):
                self.guarded(target, lambda target=target, kind=kind: self.up(kind, target).wait_send())
        self.guarded(self.me, returned)


def kernel(nx, ny, lx, ly, nh, *refs):
    field, cond_x, cond_y, weight = refs[:4]
    out, refs = refs[4:4 + nh], refs[4 + nh - 5:]
    F, KX, KY, R, RY, HALF, HT, xh, ys, yh, ch, dl = refs[5:17]
    in_sem, halo_send, halo_recv = refs[17:20]
    x_refs, y_refs = refs[20:28], refs[28:36]
    rtx, rty = ly // ROWS, lx // ROWS
    mx, my = lax.axis_index("gx"), lax.axis_index("gy")
    X = Sweep("gx", nx, nh * rtx, x_refs)
    Y = Sweep("gy", ny, nh * rty, y_refs)

    around = [(-1, 0), (1, 0), (0, -1), (0, 1), (-1, -1), (-1, 1), (1, -1), (1, 1)]

    def exists(dx, dy):
        there = None
        for d, m, n in ((dx, mx, nx), (dy, my, ny)):
            if d:
                ok = (m > 0) if d < 0 else (m < n - 1)
                there = ok if there is None else jnp.logical_and(there, ok)
        return there

    barrier = pltpu.get_barrier_semaphore()
    for target in X.others():
        pl.semaphore_signal(barrier, inc=1, device_id={"gx": target}, device_id_type=MESH)
    for target in Y.others():
        pl.semaphore_signal(barrier, inc=1, device_id={"gy": target}, device_id_type=MESH)
    for dx, dy in around[4:]:
        @pl.when(exists(dx, dy))
        def _(dx=dx, dy=dy):
            pl.semaphore_signal(barrier, inc=1, device_id={"gx": mx + dx, "gy": my + dy}, device_id_type=MESH)

    def lanes(h):
        return pl.ds(h * LANES, LANES)

    def load(k, h):
        src, dst = (
            (field, F.at[h, pl.ds(ly, lx * ly)]), (cond_x, KX.at[h]), (cond_y, KY.at[h]), (weight, R.at[h])
        )[k]
        return pltpu.make_async_copy(src.at[:, lanes(h)], dst, in_sem.at[k, h])

    for k in range(4):
        for h in range(nh):
            load(k, h).start()

    for h in range(nh):
        load(0, h).wait()
    for h in range(nh):
        ys[0, h] = F[h, pl.ds(ly, lx, stride=ly), :]
        ys[1, h] = F[h, pl.ds(ly + ly - 1, lx, stride=ly), :]

    def halo(k):
        dx, dy = around[k]
        if dy == 0:
            src = F.at[:, pl.ds(ly if dx < 0 else lx * ly, ly), :]
            dst = xh.at[1 if dx < 0 else 0]
        elif dx == 0:
            src = ys.at[0 if dy < 0 else 1]
            dst = yh.at[1 if dy < 0 else 0]
        else:
            src = ys.at[0 if dy < 0 else 1, :, pl.ds(0 if dx < 0 else lx - ROWS, ROWS), :]
            dst = ch.at[2 * (1 if dy < 0 else 0) + (1 if dx < 0 else 0)]
        return pltpu.make_async_remote_copy(
            src_ref=src,
            dst_ref=dst,
            send_sem=halo_send.at[k],
            recv_sem=halo_recv.at[around.index((-dx, -dy))],
            device_id={"gx": mx + dx, "gy": my + dy},
            device_id_type=MESH,
        )

    def halo_in(k):
        dx, dy = around[k]
        if dy == 0:
            dst = xh.at[0 if dx < 0 else 1]
        elif dx == 0:
            dst = yh.at[0 if dy < 0 else 1]
        else:
            dst = ch.at[2 * (0 if dy < 0 else 1) + (0 if dx < 0 else 1)]
        return dst, lambda: pltpu.make_async_remote_copy(
            src_ref=dst,
            dst_ref=dst,
            send_sem=halo_send.at[k],
            recv_sem=halo_recv.at[k],
            device_id={"gx": mx + dx, "gy": my + dy},
            device_id_type=MESH,
        )

    diagonal = sum(jnp.where(exists(dx, dy), 1, 0) for dx, dy in around[4:])
    pl.semaphore_wait(barrier, nx - 1 + ny - 1 + diagonal)

    for k, (dx, dy) in enumerate(around):
        @pl.when(exists(dx, dy))
        def _(k=k):
            halo(k).start()

    def rows(i, n):
        return pl.ds(pl.multiple_of(i * n, n), n)

    def put_tiles(ref, h, per_plane, values):
        for c, value in enumerate(values):
            for t in range(per_plane):
                ref[h * per_plane + t, c] = value[t * ROWS:(t + 1) * ROWS]

    def get_tiles(ref, h, per_plane, c):
        return jnp.concatenate([ref[h * per_plane + t, c] for t in range(per_plane)], axis=0)

    def send_part(sweep, h):
        if sweep.owners % nh == 0:
            sweep.send(1, h, nh)
        elif h == nh - 1:
            sweep.send(1)

    def receive_part(sweep, h):
        if sweep.owners % nh == 0:
            sweep.receive(h, nh)
        elif h == 0:
            sweep.receive(0, 1)

    for k in (1,):
        for h in range(nh):
            load(k, h).wait()

    def transfer(length, width, resistance_at):
        def steps(g, carry):
            x0, j0, x1, j1 = carry
            for r in range(ROWS):
                rho = resistance_at(g * ROWS + r)
                x0 = x0 + rho * j0
                x1 = x1 + rho * j1
                j0 = j0 + x0
                j1 = j1 + x1
            return x0, j0, x1, j1

        zero = jnp.zeros((width, LANES), jnp.float32)
        one = jnp.ones((width, LANES), jnp.float32)
        x0, j0, x1, j1 = lax.fori_loop(0, length // ROWS, steps, (one, zero, zero, one))
        return x0, x1, j0, j1

    for h in range(nh):
        def resistance_x(i, h=h):
            rho = (1.0 / step_dt) / KX[h, rows(i, ly), :]
            KX[h, rows(i, ly), :] = rho
            return rho

        put_tiles(X.t, h, rtx, transfer(lx, ly, resistance_x))
    X.send(0)

    for h in range(nh):
        load(3, h).wait()
    for k, (dx, dy) in enumerate(around):
        @pl.when(exists(dx, dy))
        def _(k=k):
            halo_in(k)[1]().wait_recv()

        @pl.when(jnp.logical_not(exists(dx, dy)))
        def _(k=k):
            dst = halo_in(k)[0]
            dst[...] = jnp.zeros(dst.shape, jnp.float32)

    for h in range(nh):
        F[h, pl.ds(0, ly), :] = xh[0, h]
        F[h, pl.ds((lx + 1) * ly, ly), :] = xh[1, h]
        for side in range(2):
            edge = yh[side, h]
            before = jnp.concatenate([ch[2 * side, h, ROWS - 1:, :], edge[:-1]], axis=0)
            after = jnp.concatenate([edge[1:], ch[2 * side + 1, h, :1, :]], axis=0)
            dl[side, h] = after - before

    row = lax.broadcasted_iota(jnp.int32, (ly, LANES), 0)
    for h in range(nh):
        def steps(g, carry, h=h):
            x, j = carry
            low = dl[0, h, rows(g, ROWS), :]
            high = dl[1, h, rows(g, ROWS), :]
            for r in range(ROWS):
                i = g * ROWS + r
                across = F[h, rows(i + 2, ly), :] - F[h, rows(i, ly), :]
                above = jnp.where(row == ly - 1, high[r:r + 1], pltpu.roll(across, ly - 1, 0))
                below = jnp.where(row == 0, low[r:r + 1], pltpu.roll(across, 1, 0))
                source = F[h, rows(i + 1, ly), :] + R[h, rows(i, ly), :] * (above - below) * 0.25
                R[h, rows(i, ly), :] = source
                x = x + KX[h, rows(i, ly), :] * j
                j = j + (x - source)
            return x, j

        zero = jnp.zeros((ly, LANES), jnp.float32)
        put_tiles(X.b, h, rtx, lax.fori_loop(0, lx // ROWS, steps, (zero, zero)))
        send_part(X, h)
    X.prepare()

    for h in range(nh):
        load(2, h).wait()
    for h in range(nh):
        def resistance_y(i, h=h):
            rho = (1.0 / step_dt) / KY[h, pl.ds(i, lx, stride=ly), :]
            RY[h, rows(i, lx), :] = rho
            return rho

        put_tiles(Y.t, h, rty, transfer(ly, lx, resistance_y))
    Y.send(0)

    X.solve()
    Y.prepare()

    for h in range(nh):
        receive_part(X, h)

        def steps(g, carry, h=h):
            x, j = carry
            for r in range(ROWS):
                i = g * ROWS + r
                x = x + KX[h, rows(i, ly), :] * j
                j = j + (x - R[h, rows(i, ly), :])
                HALF[h, rows(i, ly), :] = x
            return x, j

        start = (get_tiles(X.rs, h, rtx, 0), get_tiles(X.rs, h, rtx, 1))
        lax.fori_loop(0, lx // ROWS, steps, start)

        def steps_y(g, carry, h=h):
            x, j = carry
            for r in range(ROWS):
                i = g * ROWS + r
                half = HALF[h, pl.ds(i, lx, stride=ly), :]
                HT[h, rows(i, lx), :] = half
                x = x + RY[h, rows(i, lx), :] * j
                j = j + (x - half)
            return x, j

        zero = jnp.zeros((lx, LANES), jnp.float32)
        put_tiles(Y.b, h, rty, lax.fori_loop(0, ly // ROWS, steps_y, (zero, zero)))
        send_part(Y, h)

    for k, (dx, dy) in enumerate(around):
        @pl.when(exists(dx, dy))
        def _(k=k):
            halo(k).wait_send()
    X.drain()
    Y.solve()

    for h in range(nh):
        receive_part(Y, h)

        def steps(g, carry, h=h):
            x, j = carry
            for r in range(ROWS):
                i = g * ROWS + r
                x = x + RY[h, rows(i, lx), :] * j
                j = j + (x - HT[h, rows(i, lx), :])
                out[h][pl.ds(i, lx, stride=ly), :] = x
            return x, j

        start = (get_tiles(Y.rs, h, rty, 0), get_tiles(Y.rs, h, rty, 1))
        lax.fori_loop(0, ly // ROWS, steps, start)

    Y.drain()


def sweep_scratch(count, tiles):
    per, owners = split_tiles(tiles, count)
    return [
        pltpu.VMEM((tiles, 4, ROWS, LANES), jnp.float32),
        pltpu.VMEM((count, per, 4, ROWS, LANES), jnp.float32),
        pltpu.VMEM((tiles, 2, ROWS, LANES), jnp.float32),
        pltpu.VMEM((count, per, 2, ROWS, LANES), jnp.float32),
        pltpu.VMEM((count, per, 2, ROWS, LANES), jnp.float32),
        pltpu.VMEM((tiles, 2, ROWS, LANES), jnp.float32),
        pltpu.VMEM((count + 1, per, 2, ROWS, LANES), jnp.float32),
        pltpu.SemaphoreType.DMA((6, count)),
    ]


def shards(nx, ny, field, cond_x, cond_y, cross_weight):
    lx, ly, nz = field.shape
    nh = nz // LANES
    cells = (nh, lx * ly, LANES)
    flat = [
        pltpu.with_memory_space_constraint(a.reshape(lx * ly, nz), pltpu.HBM)
        for a in (field, cond_x, cond_y, cross_weight)
    ]
    scratch = [
        pltpu.VMEM((nh, (lx + 2) * ly, LANES), jnp.float32),
        *[pltpu.VMEM(cells, jnp.float32)] * 6,
        pltpu.VMEM((2, nh, ly, LANES), jnp.float32),
        pltpu.VMEM((2, nh, lx, LANES), jnp.float32),
        pltpu.VMEM((2, nh, lx, LANES), jnp.float32),
        pltpu.VMEM((4, nh, ROWS, LANES), jnp.float32),
        pltpu.VMEM((2, nh, lx, LANES), jnp.float32),
        pltpu.SemaphoreType.DMA((4, nh)),
        pltpu.SemaphoreType.DMA((8,)),
        pltpu.SemaphoreType.DMA((8,)),
        *sweep_scratch(nx, nh * ly // ROWS),
        *sweep_scratch(ny, nh * lx // ROWS),
    ]
    result = pl.pallas_call(
        functools.partial(kernel, nx, ny, lx, ly, nh),
        out_shape=[pltpu.VMEM(cells[1:], jnp.float32)] * nh,
        in_specs=[pl.BlockSpec(memory_space=pltpu.HBM)] * 4,
        out_specs=[pl.BlockSpec(memory_space=pltpu.VMEM)] * nh,
        scratch_shapes=scratch,
        compiler_params=pltpu.CompilerParams(
            collective_id=0, has_side_effects=True, vmem_limit_bytes=40 * 1024 * 1024
        ),
        cost_estimate=pl.CostEstimate(
            flops=60 * lx * ly * nz, bytes_accessed=20 * lx * ly * nz, transcendentals=0
        ),
        name="adi_step",
    )(*flat)
    return jnp.concatenate(result, axis=1).reshape(lx, ly, nz)


def solution(mesh):
    spec = P("gx", "gy", None)
    return jax.shard_map(
        functools.partial(shards, mesh.shape["gx"], mesh.shape["gy"]),
        mesh=mesh,
        in_specs=(spec,) * 4,
        out_specs=spec,
        check_vma=False,
    )
```

```python
import functools
import jax
import jax.numpy as jnp
from jax import lax
from jax.sharding import PartitionSpec as P
from jax.experimental import pallas as pl
from jax.experimental.pallas import tpu as pltpu

step_dt = 16384.0
LANES = 128
ROWS = 8
MESH = pl.DeviceIdType.MESH


def split_tiles(tiles, count):
    per_owner = next(p for p in range(1, tiles + 1) if tiles % p == 0 and p * count >= tiles)
    return per_owner, tiles // per_owner


class Sweep:
    def __init__(self, axis, count, tiles, parts, refs):
        self.axis, self.count, self.tiles = axis, count, tiles
        self.per, self.owners = split_tiles(tiles, count)
        self.parts = parts if self.owners % parts == 0 else 1
        (self.t, self.rt, self.b, self.rb, self.s, self.rs, self.pe, self.up_sems, self.back_sems) = refs
        self.me = lax.axis_index(axis)

    def others(self):
        return [lax.rem(self.me + d, self.count) for d in range(1, self.count)]

    def own(self):
        return pl.ds(self.me * self.per, self.per)

    def bounds(self, part):
        return self.owners * part // self.parts, self.owners * (part + 1) // self.parts

    def within(self, index, low, high, body):
        if low == 0 and high == self.count:
            body()
        elif low == 0:
            pl.when(index < high)(body)
        elif high == self.count:
            pl.when(index >= low)(body)
        else:
            pl.when(jnp.logical_and(index >= low, index < high))(body)

    def guarded(self, index, body):
        self.within(index, 0, self.owners, body)

    def copy(self, src, dst, send_sem, recv_sem, target):
        return pltpu.make_async_remote_copy(
            src_ref=src,
            dst_ref=dst,
            send_sem=send_sem,
            recv_sem=recv_sem,
            device_id={self.axis: target},
            device_id_type=MESH,
        )

    def buffers(self, kind):
        return ((self.t, self.rt), (self.b, self.rb))[kind]

    def up(self, kind, src, dst, target):
        return self.copy(src, dst, self.up_sems.at[kind, 0], self.up_sems.at[kind, 1], target)

    def send(self, kind, part=None):
        low, high = (0, self.owners) if part is None else self.bounds(part)
        mine, there = self.buffers(kind)

        def start(target):
            self.up(kind, mine.at[pl.ds(target * self.per, self.per)], there.at[self.me], target).start()

        def keep():
            there[self.me] = mine[self.own()]

        for target in self.others():
            self.within(target, low, high, lambda target=target: start(target))
        self.within(self.me, low, high, keep)

    def arrived(self, kind):
        there = self.buffers(kind)[1].at[pl.ds(0, self.count - 1)]
        self.up(kind, there, there, self.others()[0]).wait_recv()

    def prepare(self):
        def body():
            self.arrived(0)
            resistance = jnp.zeros((self.per, ROWS, LANES), jnp.float32)
            for j in range(self.count):
                inverse = 1.0 / (self.rt[j, :, 2] * resistance + self.rt[j, :, 3])
                self.pe[j, :, 0] = resistance
                self.pe[j, :, 1] = inverse
                resistance = (self.rt[j, :, 0] * resistance + self.rt[j, :, 1]) * inverse
            self.pe[self.count, :, 0] = resistance

        self.guarded(self.me, body)

    def back(self, src, dst, part, target):
        return self.copy(src, dst, self.back_sems.at[0], self.back_sems.at[1 + part], target)

    def solve(self):
        part = lax.div(self.me, self.owners // self.parts)

        def body():
            self.arrived(1)
            offset = jnp.zeros((self.per, ROWS, LANES), jnp.float32)
            offsets = []
            for j in range(self.count):
                offsets.append(offset)
                offset = offset * self.pe[j, :, 1] + (self.rb[j, :, 0] - self.pe[j + 1, :, 0] * self.rb[j, :, 1])
            flux = jnp.zeros((self.per, ROWS, LANES), jnp.float32)
            for j in reversed(range(self.count)):
                share = (self.rt[j, :, 2] * offsets[j] + self.rb[j, :, 1]) * self.pe[j, :, 1]
                flux = flux * self.pe[j, :, 1] - share
                self.s[j, :, 0] = self.pe[j, :, 0] * flux + offsets[j]
                self.s[j, :, 1] = flux
            for target in self.others():
                self.back(self.s.at[target], self.rs.at[self.own()], part, target).start()
            self.rs[self.own()] = self.s[self.me]

        self.guarded(self.me, body)

    def receive(self, part):
        if part >= self.parts:
            return
        low, high = self.bounds(part)

        def wait(owners):
            if owners:
                there = self.rs.at[pl.ds(0, owners * self.per)]
                self.back(there, there, part, self.others()[0]).wait_recv()

        inside = jnp.logical_and(self.me >= low, self.me < high)
        pl.when(inside)(lambda: wait(high - low - 1))
        pl.when(jnp.logical_not(inside))(lambda: wait(high - low))

    def drain(self):
        def sent(owners):
            for kind in (0, 1):
                if owners:
                    mine = self.buffers(kind)[0].at[pl.ds(0, owners * self.per)]
                    self.up(kind, mine, mine, self.others()[0]).wait_send()

        def owner():
            sent(self.owners - 1)
            mine = self.s.at[pl.ds(0, self.count - 1)]
            self.back(mine, mine, 0, self.others()[0]).wait_send()

        self.guarded(self.me, owner)
        if self.owners < self.count:
            pl.when(self.me >= self.owners)(lambda: sent(self.owners))


def kernel(nx, ny, lx, ly, nh, pitch, *refs):
    field, cond_x, cond_y, weight = refs[:4]
    out, refs = refs[4:4 + nh], refs[4 + nh - 5:]
    F, KX, KY, R, RY, HALF, HT, xh, ys, yh, ch, dl = refs[5:17]
    in_sem, halo_send, halo_recv = refs[17:20]
    x_refs, y_refs = refs[20:29], refs[29:38]
    rtx, rty = ly // ROWS, lx // ROWS
    mx, my = lax.axis_index("gx"), lax.axis_index("gy")
    X = Sweep("gx", nx, nh * rtx, nh, x_refs)
    Y = Sweep("gy", ny, nh * rty, nh, y_refs)

    around = [(-1, 0), (1, 0), (0, -1), (0, 1), (-1, -1), (-1, 1), (1, -1), (1, 1)]

    def exists(dx, dy):
        there = None
        for d, m, n in ((dx, mx, nx), (dy, my, ny)):
            if d:
                ok = (m > 0) if d < 0 else (m < n - 1)
                there = ok if there is None else jnp.logical_and(there, ok)
        return there

    barrier = pltpu.get_barrier_semaphore()
    for target in X.others():
        pl.semaphore_signal(barrier, inc=1, device_id={"gx": target}, device_id_type=MESH)
    for target in Y.others():
        pl.semaphore_signal(barrier, inc=1, device_id={"gy": target}, device_id_type=MESH)
    for dx, dy in around[4:]:
        @pl.when(exists(dx, dy))
        def _(dx=dx, dy=dy):
            pl.semaphore_signal(barrier, inc=1, device_id={"gx": mx + dx, "gy": my + dy}, device_id_type=MESH)

    def lanes(h):
        return pl.ds(h * LANES, LANES)

    def load(k, h):
        src, dst = (
            (field, F.at[h, pl.ds(ly, lx * ly)]), (cond_x, KX.at[h]), (cond_y, KY.at[h]), (weight, R.at[h])
        )[k]
        return pltpu.make_async_copy(src.at[:, lanes(h)], dst, in_sem.at[k, h])

    def start(k):
        for h in range(nh):
            load(k, h).start()

    start(0)
    start(1)

    for h in range(nh):
        load(0, h).wait()
    start(3)
    for h in range(nh):
        ys[0, h] = F[h, pl.ds(ly, lx, stride=ly), :]
        ys[1, h] = F[h, pl.ds(ly + ly - 1, lx, stride=ly), :]

    def halo(k):
        dx, dy = around[k]
        if dy == 0:
            src = F.at[:, pl.ds(ly if dx < 0 else lx * ly, ly), :]
            dst = xh.at[1 if dx < 0 else 0]
        elif dx == 0:
            src = ys.at[0 if dy < 0 else 1]
            dst = yh.at[1 if dy < 0 else 0]
        else:
            src = ys.at[0 if dy < 0 else 1, :, pl.ds(0 if dx < 0 else lx - ROWS, ROWS), :]
            dst = ch.at[2 * (1 if dy < 0 else 0) + (1 if dx < 0 else 0)]
        return pltpu.make_async_remote_copy(
            src_ref=src,
            dst_ref=dst,
            send_sem=halo_send.at[k],
            recv_sem=halo_recv.at[around.index((-dx, -dy))],
            device_id={"gx": mx + dx, "gy": my + dy},
            device_id_type=MESH,
        )

    def halo_in(k):
        dx, dy = around[k]
        if dy == 0:
            dst = xh.at[0 if dx < 0 else 1]
        elif dx == 0:
            dst = yh.at[0 if dy < 0 else 1]
        else:
            dst = ch.at[2 * (0 if dy < 0 else 1) + (0 if dx < 0 else 1)]
        return dst, lambda: pltpu.make_async_remote_copy(
            src_ref=dst,
            dst_ref=dst,
            send_sem=halo_send.at[k],
            recv_sem=halo_recv.at[k],
            device_id={"gx": mx + dx, "gy": my + dy},
            device_id_type=MESH,
        )

    diagonal = sum(jnp.where(exists(dx, dy), 1, 0) for dx, dy in around[4:])
    pl.semaphore_wait(barrier, nx - 1 + ny - 1 + diagonal)

    for k, (dx, dy) in enumerate(around):
        @pl.when(exists(dx, dy))
        def _(k=k):
            halo(k).start()

    for k, (dx, dy) in enumerate(around):
        @pl.when(jnp.logical_not(exists(dx, dy)))
        def _(k=k):
            dst = halo_in(k)[0]
            dst[...] = jnp.zeros(dst.shape, jnp.float32)

    def rows(i, n):
        return pl.ds(pl.multiple_of(i * n, n), n)

    def put_tiles(ref, h, per_plane, values):
        for c, value in enumerate(values):
            for t in range(per_plane):
                ref[h * per_plane + t, c] = value[t * ROWS:(t + 1) * ROWS]

    def get_tiles(ref, h, per_plane, c):
        return jnp.concatenate([ref[h * per_plane + t, c] for t in range(per_plane)], axis=0)

    def send_part(sweep, h):
        if sweep.parts == nh:
            sweep.send(1, h)
        elif h == nh - 1:
            sweep.send(1)

    def transfer(length, width, resistance_at):
        def steps(g, carry):
            x0, j0, x1, j1 = carry
            for r in range(ROWS):
                rho = resistance_at(g * ROWS + r)
                x0 = x0 + rho * j0
                x1 = x1 + rho * j1
                j0 = j0 + x0
                j1 = j1 + x1
            return x0, j0, x1, j1

        zero = jnp.zeros((width, LANES), jnp.float32)
        one = jnp.ones((width, LANES), jnp.float32)
        x0, j0, x1, j1 = lax.fori_loop(0, length // ROWS, steps, (one, zero, zero, one))
        return x0, x1, j0, j1

    for h in range(nh):
        load(1, h).wait()
        if h == nh - 1:
            start(2)

        def resistance_x(i, h=h):
            rho = (1.0 / step_dt) / KX[h, rows(i, ly), :]
            KX[h, rows(i, ly), :] = rho
            return rho

        put_tiles(X.t, h, rtx, transfer(lx, ly, resistance_x))
    X.send(0)

    for k, (dx, dy) in enumerate(around):
        @pl.when(exists(dx, dy))
        def _(k=k):
            halo_in(k)[1]().wait_recv()

    for h in range(nh):
        F[h, pl.ds(0, ly), :] = xh[0, h]
        F[h, pl.ds((lx + 1) * ly, ly), :] = xh[1, h]
        for side in range(2):
            edge = yh[side, h]
            before = jnp.concatenate([ch[2 * side, h, ROWS - 1:, :], edge[:-1]], axis=0)
            after = jnp.concatenate([edge[1:], ch[2 * side + 1, h, :1, :]], axis=0)
            dl[side, h] = after - before

    row = lax.broadcasted_iota(jnp.int32, (ly, LANES), 0)
    for h in range(nh):
        load(3, h).wait()

        def steps(g, carry, h=h):
            x, j = carry
            low = dl[0, h, rows(g, ROWS), :]
            high = dl[1, h, rows(g, ROWS), :]
            for r in range(ROWS):
                i = g * ROWS + r
                across = F[h, rows(i + 2, ly), :] - F[h, rows(i, ly), :]
                above = jnp.where(row == ly - 1, high[r:r + 1], pltpu.roll(across, ly - 1, 0))
                below = jnp.where(row == 0, low[r:r + 1], pltpu.roll(across, 1, 0))
                source = F[h, rows(i + 1, ly), :] + R[h, rows(i, ly), :] * (above - below) * 0.25
                R[h, rows(i, ly), :] = source
                x = x + KX[h, rows(i, ly), :] * j
                j = (j - source) + x
            return x, j

        zero = jnp.zeros((ly, LANES), jnp.float32)
        put_tiles(X.b, h, rtx, lax.fori_loop(0, lx // ROWS, steps, (zero, zero)))
        send_part(X, h)
    X.prepare()

    for h in range(nh):
        load(2, h).wait()

        def resistance_y(i, h=h):
            rho = (1.0 / step_dt) / KY[h, pl.ds(i, lx, stride=ly), :]
            RY[h, rows(i, lx), :] = rho
            return rho

        put_tiles(Y.t, h, rty, transfer(ly, lx, resistance_y))
    Y.send(0)

    X.solve()
    Y.prepare()

    for h in range(nh):
        X.receive(h)

        def steps(g, carry, h=h):
            x, j = carry
            for r in range(ROWS):
                i = g * ROWS + r
                x = x + KX[h, rows(i, ly), :] * j
                j = (j - R[h, rows(i, ly), :]) + x
                HALF[h, pl.ds(pl.multiple_of(i * pitch, ROWS), ly), :] = x
            return x, j

        start = (get_tiles(X.rs, h, rtx, 0), get_tiles(X.rs, h, rtx, 1))
        lax.fori_loop(0, lx // ROWS, steps, start)

        def steps_y(g, carry, h=h):
            x, j = carry
            for r in range(ROWS):
                i = g * ROWS + r
                half = HALF[h, pl.ds(i, lx, stride=pitch), :]
                HT[h, rows(i, lx), :] = half
                x = x + RY[h, rows(i, lx), :] * j
                j = (j - half) + x
            return x, j

        zero = jnp.zeros((lx, LANES), jnp.float32)
        put_tiles(Y.b, h, rty, lax.fori_loop(0, ly // ROWS, steps_y, (zero, zero)))
        send_part(Y, h)

    for k, (dx, dy) in enumerate(around):
        @pl.when(exists(dx, dy))
        def _(k=k):
            halo(k).wait_send()
    X.drain()
    Y.solve()

    for h in range(nh):
        Y.receive(h)

        def steps(g, carry, h=h):
            x, j = carry
            for r in range(ROWS):
                i = g * ROWS + r
                x = x + RY[h, rows(i, lx), :] * j
                j = (j - HT[h, rows(i, lx), :]) + x
                out[h][pl.ds(i, lx, stride=ly), :] = x
            return x, j

        start = (get_tiles(Y.rs, h, rty, 0), get_tiles(Y.rs, h, rty, 1))
        lax.fori_loop(0, ly // ROWS, steps, start)

    Y.drain()


def sweep_scratch(count, tiles, parts):
    per, owners = split_tiles(tiles, count)
    return [
        pltpu.VMEM((tiles, 4, ROWS, LANES), jnp.float32),
        pltpu.VMEM((count, per, 4, ROWS, LANES), jnp.float32),
        pltpu.VMEM((tiles, 2, ROWS, LANES), jnp.float32),
        pltpu.VMEM((count, per, 2, ROWS, LANES), jnp.float32),
        pltpu.VMEM((count, per, 2, ROWS, LANES), jnp.float32),
        pltpu.VMEM((tiles, 2, ROWS, LANES), jnp.float32),
        pltpu.VMEM((count + 1, per, 2, ROWS, LANES), jnp.float32),
        pltpu.SemaphoreType.DMA((2, 2)),
        pltpu.SemaphoreType.DMA((1 + parts,)),
    ]


def shards(nx, ny, field, cond_x, cond_y, cross_weight):
    lx, ly, nz = field.shape
    nh = nz // LANES
    cells = (nh, lx * ly, LANES)
    pitch = ly + ROWS if ly // ROWS % 2 == 0 else ly
    flat = [
        pltpu.with_memory_space_constraint(a.reshape(lx * ly, nz), pltpu.HBM)
        for a in (field, cond_x, cond_y, cross_weight)
    ]
    scratch = [
        pltpu.VMEM((nh, (lx + 2) * ly, LANES), jnp.float32),
        *[pltpu.VMEM(cells, jnp.float32)] * 4,
        pltpu.VMEM((nh, lx * pitch, LANES), jnp.float32),
        pltpu.VMEM(cells, jnp.float32),
        pltpu.VMEM((2, nh, ly, LANES), jnp.float32),
        pltpu.VMEM((2, nh, lx, LANES), jnp.float32),
        pltpu.VMEM((2, nh, lx, LANES), jnp.float32),
        pltpu.VMEM((4, nh, ROWS, LANES), jnp.float32),
        pltpu.VMEM((2, nh, lx, LANES), jnp.float32),
        pltpu.SemaphoreType.DMA((4, nh)),
        pltpu.SemaphoreType.DMA((8,)),
        pltpu.SemaphoreType.DMA((8,)),
        *sweep_scratch(nx, nh * ly // ROWS, nh),
        *sweep_scratch(ny, nh * lx // ROWS, nh),
    ]
    result = pl.pallas_call(
        functools.partial(kernel, nx, ny, lx, ly, nh, pitch),
        out_shape=[pltpu.VMEM((lx * ly, LANES), jnp.float32)] * nh,
        in_specs=[pl.BlockSpec(memory_space=pltpu.HBM)] * 4,
        out_specs=[pl.BlockSpec(memory_space=pltpu.VMEM)] * nh,
        scratch_shapes=scratch,
        compiler_params=pltpu.CompilerParams(
            collective_id=0, has_side_effects=True, vmem_limit_bytes=40 * 1024 * 1024
        ),
        cost_estimate=pl.CostEstimate(
            flops=60 * lx * ly * nz, bytes_accessed=20 * lx * ly * nz, transcendentals=0
        ),
        name="adi_step",
    )(*flat)

    return jnp.concatenate(result, axis=1).reshape(lx, ly, nz)


def solution(mesh):
    spec = P("gx", "gy", None)
    return jax.shard_map(
        functools.partial(shards, mesh.shape["gx"], mesh.shape["gy"]),
        mesh=mesh,
        in_specs=(spec,) * 4,
        out_specs=spec,
        check_vma=False,
    )
```

```python
import functools
import jax
import jax.numpy as jnp
from jax import lax
from jax.sharding import PartitionSpec as P
from jax.experimental import pallas as pl
from jax.experimental.pallas import tpu as pltpu

step_dt = 16384.0
LANES = 128
ROWS = 8
MESH = pl.DeviceIdType.MESH


def split_tiles(tiles, most):
    per_owner = next(p for p in range(1, tiles + 1) if tiles % p == 0 and p * most >= tiles)
    return per_owner, tiles // per_owner


class Sweep:
    def __init__(self, axis, count, most, tiles, parts, refs):
        self.axis, self.count, self.tiles = axis, count, tiles
        self.per, self.owners = split_tiles(tiles, most)
        self.base = (count - self.owners) // 2
        self.parts = parts if self.owners % parts == 0 else 1
        (self.t, self.rt, self.b, self.rb, self.s, self.rs, self.pe, self.up_sems, self.back_sems) = refs
        self.me = lax.axis_index(axis)

    def others(self):
        return [lax.rem(self.me + d, self.count) for d in range(1, self.count)]

    def of(self, owner):
        return pl.ds((owner - self.base) * self.per, self.per)

    def own(self):
        return self.of(self.me)

    def is_owner(self):
        return jnp.logical_and(self.me >= self.base, self.me < self.base + self.owners)

    def bounds(self, part):
        each = self.owners // self.parts
        return self.base + each * part, self.base + each * (part + 1)

    def on_owner(self, body):
        if self.owners == self.count:
            body()
        else:
            pl.when(self.is_owner())(body)

    def copy(self, src, dst, send_sem, recv_sem, target):
        return pltpu.make_async_remote_copy(
            src_ref=src,
            dst_ref=dst,
            send_sem=send_sem,
            recv_sem=recv_sem,
            device_id={self.axis: target},
            device_id_type=MESH,
        )

    def buffers(self, kind):
        return ((self.t, self.rt), (self.b, self.rb))[kind]

    def up(self, kind, src, dst, target):
        return self.copy(src, dst, self.up_sems.at[kind, 0], self.up_sems.at[kind, 1], target)

    def send(self, kind, part=None):
        low, high = (self.base, self.base + self.owners) if part is None else self.bounds(part)
        mine, there = self.buffers(kind)
        for owner in range(low, high):
            @pl.when(self.me != owner)
            def _(owner=owner):
                self.up(kind, mine.at[self.of(owner)], there.at[self.me], owner).start()

            @pl.when(self.me == owner)
            def _(owner=owner):
                there[owner] = mine[self.of(owner)]

    def arrived(self, kind):
        there = self.buffers(kind)[1].at[pl.ds(0, self.count - 1)]
        self.up(kind, there, there, self.others()[0]).wait_recv()

    def prepare(self):
        def body():
            self.arrived(0)
            resistance = jnp.zeros((self.per, ROWS, LANES), jnp.float32)
            for j in range(self.count):
                inverse = 1.0 / (self.rt[j, :, 2] * resistance + self.rt[j, :, 3])
                self.pe[j, :, 0] = resistance
                self.pe[j, :, 1] = inverse
                resistance = (self.rt[j, :, 0] * resistance + self.rt[j, :, 1]) * inverse
            self.pe[self.count, :, 0] = resistance

        self.on_owner(body)

    def back(self, src, dst, part, target):
        return self.copy(src, dst, self.back_sems.at[0], self.back_sems.at[1 + part], target)

    def solve(self):
        part = lax.div(self.me - self.base, self.owners // self.parts)

        def body():
            self.arrived(1)
            offset = jnp.zeros((self.per, ROWS, LANES), jnp.float32)
            offsets = []
            for j in range(self.count):
                offsets.append(offset)
                offset = offset * self.pe[j, :, 1] + (self.rb[j, :, 0] - self.pe[j + 1, :, 0] * self.rb[j, :, 1])
            flux = jnp.zeros((self.per, ROWS, LANES), jnp.float32)
            for j in reversed(range(self.count)):
                share = (self.rt[j, :, 2] * offsets[j] + self.rb[j, :, 1]) * self.pe[j, :, 1]
                flux = flux * self.pe[j, :, 1] - share
                self.s[j, :, 0] = self.pe[j, :, 0] * flux + offsets[j]
                self.s[j, :, 1] = flux
            for target in self.others():
                self.back(self.s.at[target], self.rs.at[self.own()], part, target).start()
            self.rs[self.own()] = self.s[self.me]

        self.on_owner(body)

    def receive(self, part):
        if part >= self.parts:
            return
        low, high = self.bounds(part)

        def wait(owners):
            if owners:
                there = self.rs.at[pl.ds(0, owners * self.per)]
                self.back(there, there, part, self.others()[0]).wait_recv()

        inside = jnp.logical_and(self.me >= low, self.me < high)
        pl.when(inside)(lambda: wait(high - low - 1))
        pl.when(jnp.logical_not(inside))(lambda: wait(high - low))

    def drain(self):
        def sent(owners):
            for kind in (0, 1):
                if owners:
                    mine = self.buffers(kind)[0].at[pl.ds(0, owners * self.per)]
                    self.up(kind, mine, mine, self.others()[0]).wait_send()

        def owner():
            sent(self.owners - 1)
            mine = self.s.at[pl.ds(0, self.count - 1)]
            self.back(mine, mine, 0, self.others()[0]).wait_send()

        self.on_owner(owner)
        if self.owners < self.count:
            pl.when(jnp.logical_not(self.is_owner()))(lambda: sent(self.owners))


def kernel(nx, ny, lx, ly, nh, pitch, *refs):
    field, cond_x, cond_y, weight = refs[:4]
    out, refs = refs[4:4 + nh], refs[4 + nh - 5:]
    F, KX, KY, R, RY, HALF, HT, xh, ys, yh, ch, dl = refs[5:17]
    in_sem, halo_send, halo_recv = refs[17:20]
    x_refs, y_refs = refs[20:29], refs[29:38]
    rtx, rty = ly // ROWS, lx // ROWS
    mx, my = lax.axis_index("gx"), lax.axis_index("gy")
    X = Sweep("gx", nx, max(1, nx // 2), nh * rtx, nh, x_refs)
    Y = Sweep("gy", ny, ny, nh * rty, nh, y_refs)

    around = [(-1, 0), (1, 0), (0, -1), (0, 1), (-1, -1), (-1, 1), (1, -1), (1, 1)]

    def exists(dx, dy):
        there = None
        for d, m, n in ((dx, mx, nx), (dy, my, ny)):
            if d:
                ok = (m > 0) if d < 0 else (m < n - 1)
                there = ok if there is None else jnp.logical_and(there, ok)
        return there

    barrier = pltpu.get_barrier_semaphore()
    for target in X.others():
        pl.semaphore_signal(barrier, inc=1, device_id={"gx": target}, device_id_type=MESH)
    for target in Y.others():
        pl.semaphore_signal(barrier, inc=1, device_id={"gy": target}, device_id_type=MESH)
    for dx, dy in around[4:]:
        @pl.when(exists(dx, dy))
        def _(dx=dx, dy=dy):
            pl.semaphore_signal(barrier, inc=1, device_id={"gx": mx + dx, "gy": my + dy}, device_id_type=MESH)

    def lanes(h):
        return pl.ds(h * LANES, LANES)

    def load(k, h):
        src, dst = (
            (field, F.at[h, pl.ds(ly, lx * ly)]), (cond_x, KX.at[h]), (cond_y, KY.at[h]), (weight, R.at[h])
        )[k]
        return pltpu.make_async_copy(src.at[:, lanes(h)], dst, in_sem.at[k, h])

    def start(k):
        for h in range(nh):
            load(k, h).start()

    start(0)
    start(1)

    for h in range(nh):
        load(0, h).wait()
    start(3)
    for h in range(nh):
        ys[0, h] = F[h, pl.ds(ly, lx, stride=ly), :]
        ys[1, h] = F[h, pl.ds(ly + ly - 1, lx, stride=ly), :]

    def halo(k):
        dx, dy = around[k]
        if dy == 0:
            src = F.at[:, pl.ds(ly if dx < 0 else lx * ly, ly), :]
            dst = xh.at[1 if dx < 0 else 0]
        elif dx == 0:
            src = ys.at[0 if dy < 0 else 1]
            dst = yh.at[1 if dy < 0 else 0]
        else:
            src = ys.at[0 if dy < 0 else 1, :, pl.ds(0 if dx < 0 else lx - ROWS, ROWS), :]
            dst = ch.at[2 * (1 if dy < 0 else 0) + (1 if dx < 0 else 0)]
        return pltpu.make_async_remote_copy(
            src_ref=src,
            dst_ref=dst,
            send_sem=halo_send.at[k],
            recv_sem=halo_recv.at[around.index((-dx, -dy))],
            device_id={"gx": mx + dx, "gy": my + dy},
            device_id_type=MESH,
        )

    def halo_in(k):
        dx, dy = around[k]
        if dy == 0:
            dst = xh.at[0 if dx < 0 else 1]
        elif dx == 0:
            dst = yh.at[0 if dy < 0 else 1]
        else:
            dst = ch.at[2 * (0 if dy < 0 else 1) + (0 if dx < 0 else 1)]
        return dst, lambda: pltpu.make_async_remote_copy(
            src_ref=dst,
            dst_ref=dst,
            send_sem=halo_send.at[k],
            recv_sem=halo_recv.at[k],
            device_id={"gx": mx + dx, "gy": my + dy},
            device_id_type=MESH,
        )

    diagonal = sum(jnp.where(exists(dx, dy), 1, 0) for dx, dy in around[4:])
    pl.semaphore_wait(barrier, nx - 1 + ny - 1 + diagonal)

    for k, (dx, dy) in enumerate(around):
        @pl.when(exists(dx, dy))
        def _(k=k):
            halo(k).start()

    for k, (dx, dy) in enumerate(around):
        @pl.when(jnp.logical_not(exists(dx, dy)))
        def _(k=k):
            dst = halo_in(k)[0]
            dst[...] = jnp.zeros(dst.shape, jnp.float32)

    def rows(i, n):
        return pl.ds(pl.multiple_of(i * n, n), n)

    def put_tiles(ref, h, per_plane, values):
        for c, value in enumerate(values):
            for t in range(per_plane):
                ref[h * per_plane + t, c] = value[t * ROWS:(t + 1) * ROWS]

    def get_tiles(ref, h, per_plane, c):
        return jnp.concatenate([ref[h * per_plane + t, c] for t in range(per_plane)], axis=0)

    def send_part(sweep, h):
        if sweep.parts == nh:
            sweep.send(1, h)
        elif h == nh - 1:
            sweep.send(1)

    def transfer(length, width, resistance_at):
        def steps(g, carry):
            x0, j0, x1, j1 = carry
            for r in range(ROWS):
                rho = resistance_at(g * ROWS + r)
                x0 = x0 + rho * j0
                x1 = x1 + rho * j1
                j0 = j0 + x0
                j1 = j1 + x1
            return x0, j0, x1, j1

        zero = jnp.zeros((width, LANES), jnp.float32)
        one = jnp.ones((width, LANES), jnp.float32)
        x0, j0, x1, j1 = lax.fori_loop(0, length // ROWS, steps, (one, zero, zero, one))
        return x0, x1, j0, j1

    for h in range(nh):
        load(1, h).wait()
        if h == nh - 1:
            start(2)

        def resistance_x(i, h=h):
            rho = (1.0 / step_dt) / KX[h, rows(i, ly), :]
            KX[h, rows(i, ly), :] = rho
            return rho

        put_tiles(X.t, h, rtx, transfer(lx, ly, resistance_x))
    X.send(0)

    for k, (dx, dy) in enumerate(around):
        @pl.when(exists(dx, dy))
        def _(k=k):
            halo_in(k)[1]().wait_recv()

    for h in range(nh):
        F[h, pl.ds(0, ly), :] = xh[0, h]
        F[h, pl.ds((lx + 1) * ly, ly), :] = xh[1, h]
        for side in range(2):
            edge = yh[side, h]
            before = jnp.concatenate([ch[2 * side, h, ROWS - 1:, :], edge[:-1]], axis=0)
            after = jnp.concatenate([edge[1:], ch[2 * side + 1, h, :1, :]], axis=0)
            dl[side, h] = after - before

    row = lax.broadcasted_iota(jnp.int32, (ly, LANES), 0)
    for h in range(nh):
        load(3, h).wait()

        def steps(g, carry, h=h):
            x, j = carry
            low = dl[0, h, rows(g, ROWS), :]
            high = dl[1, h, rows(g, ROWS), :]
            for r in range(ROWS):
                i = g * ROWS + r
                across = F[h, rows(i + 2, ly), :] - F[h, rows(i, ly), :]
                above = jnp.where(row == ly - 1, high[r:r + 1], pltpu.roll(across, ly - 1, 0))
                below = jnp.where(row == 0, low[r:r + 1], pltpu.roll(across, 1, 0))
                source = F[h, rows(i + 1, ly), :] + R[h, rows(i, ly), :] * (above - below) * 0.25
                R[h, rows(i, ly), :] = source
                x = x + KX[h, rows(i, ly), :] * j
                j = (j - source) + x
            return x, j

        zero = jnp.zeros((ly, LANES), jnp.float32)
        put_tiles(X.b, h, rtx, lax.fori_loop(0, lx // ROWS, steps, (zero, zero)))
        send_part(X, h)
    X.prepare()

    for h in range(nh):
        load(2, h).wait()

        def resistance_y(i, h=h):
            rho = (1.0 / step_dt) / KY[h, pl.ds(i, lx, stride=ly), :]
            RY[h, rows(i, lx), :] = rho
            return rho

        put_tiles(Y.t, h, rty, transfer(ly, lx, resistance_y))
    Y.send(0)

    X.solve()
    Y.prepare()

    for h in range(nh):
        X.receive(h)

        def steps(g, carry, h=h):
            x, j = carry
            for r in range(ROWS):
                i = g * ROWS + r
                x = x + KX[h, rows(i, ly), :] * j
                j = (j - R[h, rows(i, ly), :]) + x
                HALF[h, pl.ds(pl.multiple_of(i * pitch, ROWS), ly), :] = x
            return x, j

        start = (get_tiles(X.rs, h, rtx, 0), get_tiles(X.rs, h, rtx, 1))
        lax.fori_loop(0, lx // ROWS, steps, start)

        def steps_y(g, carry, h=h):
            x, j = carry
            for r in range(ROWS):
                i = g * ROWS + r
                half = HALF[h, pl.ds(i, lx, stride=pitch), :]
                HT[h, rows(i, lx), :] = half
                x = x + RY[h, rows(i, lx), :] * j
                j = (j - half) + x
            return x, j

        zero = jnp.zeros((lx, LANES), jnp.float32)
        put_tiles(Y.b, h, rty, lax.fori_loop(0, ly // ROWS, steps_y, (zero, zero)))
        send_part(Y, h)

    for k, (dx, dy) in enumerate(around):
        @pl.when(exists(dx, dy))
        def _(k=k):
            halo(k).wait_send()
    X.drain()
    Y.solve()

    for h in range(nh):
        Y.receive(h)

        def steps(g, carry, h=h):
            x, j = carry
            for r in range(ROWS):
                i = g * ROWS + r
                x = x + RY[h, rows(i, lx), :] * j
                j = (j - HT[h, rows(i, lx), :]) + x
                HALF[h, pl.ds(i, lx, stride=pitch), :] = x
            return x, j

        start = (get_tiles(Y.rs, h, rty, 0), get_tiles(Y.rs, h, rty, 1))
        lax.fori_loop(0, ly // ROWS, steps, start)

        def planes(g, carry, h=h):
            for r in range(ROWS):
                i = g * ROWS + r
                out[h][rows(i, ly), :] = HALF[h, pl.ds(pl.multiple_of(i * pitch, ROWS), ly), :]
            return carry

        lax.fori_loop(0, lx // ROWS, planes, 0)

    Y.drain()


def sweep_scratch(count, most, tiles, parts):
    per, owners = split_tiles(tiles, most)
    return [
        pltpu.VMEM((tiles, 4, ROWS, LANES), jnp.float32),
        pltpu.VMEM((count, per, 4, ROWS, LANES), jnp.float32),
        pltpu.VMEM((tiles, 2, ROWS, LANES), jnp.float32),
        pltpu.VMEM((count, per, 2, ROWS, LANES), jnp.float32),
        pltpu.VMEM((count, per, 2, ROWS, LANES), jnp.float32),
        pltpu.VMEM((tiles, 2, ROWS, LANES), jnp.float32),
        pltpu.VMEM((count + 1, per, 2, ROWS, LANES), jnp.float32),
        pltpu.SemaphoreType.DMA((2, 2)),
        pltpu.SemaphoreType.DMA((1 + parts,)),
    ]


def shards(nx, ny, field, cond_x, cond_y, cross_weight):
    lx, ly, nz = field.shape
    nh = nz // LANES
    cells = (nh, lx * ly, LANES)
    pitch = ly + ROWS if ly // ROWS % 2 == 0 else ly
    flat = [
        pltpu.with_memory_space_constraint(a.reshape(lx * ly, nz), pltpu.HBM)
        for a in (field, cond_x, cond_y, cross_weight)
    ]
    scratch = [
        pltpu.VMEM((nh, (lx + 2) * ly, LANES), jnp.float32),
        *[pltpu.VMEM(cells, jnp.float32)] * 4,
        pltpu.VMEM((nh, lx * pitch, LANES), jnp.float32),
        pltpu.VMEM(cells, jnp.float32),
        pltpu.VMEM((2, nh, ly, LANES), jnp.float32),
        pltpu.VMEM((2, nh, lx, LANES), jnp.float32),
        pltpu.VMEM((2, nh, lx, LANES), jnp.float32),
        pltpu.VMEM((4, nh, ROWS, LANES), jnp.float32),
        pltpu.VMEM((2, nh, lx, LANES), jnp.float32),
        pltpu.SemaphoreType.DMA((4, nh)),
        pltpu.SemaphoreType.DMA((8,)),
        pltpu.SemaphoreType.DMA((8,)),
        *sweep_scratch(nx, max(1, nx // 2), nh * ly // ROWS, nh),
        *sweep_scratch(ny, ny, nh * lx // ROWS, nh),
    ]
    result = pl.pallas_call(
        functools.partial(kernel, nx, ny, lx, ly, nh, pitch),
        out_shape=[pltpu.VMEM((lx * ly, LANES), jnp.float32)] * nh,
        in_specs=[pl.BlockSpec(memory_space=pltpu.HBM)] * 4,
        out_specs=[pl.BlockSpec(memory_space=pltpu.VMEM)] * nh,
        scratch_shapes=scratch,
        compiler_params=pltpu.CompilerParams(
            collective_id=0, has_side_effects=True, vmem_limit_bytes=40 * 1024 * 1024
        ),
        cost_estimate=pl.CostEstimate(
            flops=60 * lx * ly * nz, bytes_accessed=20 * lx * ly * nz, transcendentals=0
        ),
        name="adi_step",
    )(*flat)
    return jnp.concatenate(result, axis=1).reshape(lx, ly, nz)


def solution(mesh):
    spec = P("gx", "gy", None)
    return jax.shard_map(
        functools.partial(shards, mesh.shape["gx"], mesh.shape["gy"]),
        mesh=mesh,
        in_specs=(spec,) * 4,
        out_specs=spec,
        check_vma=False,
    )
```

```python
import functools
import jax
import jax.numpy as jnp
from jax import lax
from jax.sharding import PartitionSpec as P
from jax.experimental import pallas as pl
from jax.experimental.pallas import tpu as pltpu

step_dt = 16384.0
LANES = 128
ROWS = 8
MESH = pl.DeviceIdType.MESH


def split_tiles(tiles, most):
    per_owner = next(p for p in range(1, tiles + 1) if tiles % p == 0 and p * most >= tiles)
    return per_owner, tiles // per_owner


class Sweep:
    def __init__(self, axis, count, most, tiles, parts, refs):
        self.axis, self.count, self.tiles = axis, count, tiles
        self.per, self.owners = split_tiles(tiles, most)
        self.base = (count - self.owners) // 2
        self.parts = parts if self.owners % parts == 0 else 1
        (self.t, self.rt, self.b, self.rb, self.s, self.rs, self.pe, self.up_sems, self.back_sems) = refs
        self.me = lax.axis_index(axis)

    def others(self):
        return [lax.rem(self.me + d, self.count) for d in range(1, self.count)]

    def of(self, owner):
        return pl.ds((owner - self.base) * self.per, self.per)

    def own(self):
        return self.of(self.me)

    def is_owner(self):
        return jnp.logical_and(self.me >= self.base, self.me < self.base + self.owners)

    def bounds(self, part):
        each = self.owners // self.parts
        return self.base + each * part, self.base + each * (part + 1)

    def on_owner(self, body):
        if self.owners == self.count:
            body()
        else:
            pl.when(self.is_owner())(body)

    def copy(self, src, dst, send_sem, recv_sem, target):
        return pltpu.make_async_remote_copy(
            src_ref=src,
            dst_ref=dst,
            send_sem=send_sem,
            recv_sem=recv_sem,
            device_id={self.axis: target},
            device_id_type=MESH,
        )

    def buffers(self, kind):
        return ((self.t, self.rt), (self.b, self.rb))[kind]

    def up(self, kind, src, dst, target):
        return self.copy(src, dst, self.up_sems.at[kind, 0], self.up_sems.at[kind, 1], target)

    def send(self, kind, part=None):
        low, high = (self.base, self.base + self.owners) if part is None else self.bounds(part)
        mine, there = self.buffers(kind)
        for owner in range(low, high):
            @pl.when(self.me != owner)
            def _(owner=owner):
                self.up(kind, mine.at[self.of(owner)], there.at[self.me], owner).start()

            @pl.when(self.me == owner)
            def _(owner=owner):
                there[owner] = mine[self.of(owner)]

    def arrived(self, kind):
        there = self.buffers(kind)[1].at[pl.ds(0, self.count - 1)]
        self.up(kind, there, there, self.others()[0]).wait_recv()

    def prepare(self):
        def body():
            self.arrived(0)
            resistance = jnp.zeros((self.per, ROWS, LANES), jnp.float32)
            for j in range(self.count):
                inverse = 1.0 / (self.rt[j, :, 2] * resistance + self.rt[j, :, 3])
                self.pe[j, :, 0] = resistance
                self.pe[j, :, 1] = inverse
                resistance = (self.rt[j, :, 0] * resistance + self.rt[j, :, 1]) * inverse
            self.pe[self.count, :, 0] = resistance

        self.on_owner(body)

    def back(self, src, dst, part, target):
        return self.copy(src, dst, self.back_sems.at[0], self.back_sems.at[1 + part], target)

    def solve(self):
        part = lax.div(self.me - self.base, self.owners // self.parts)

        def body():
            self.arrived(1)
            offset = jnp.zeros((self.per, ROWS, LANES), jnp.float32)
            offsets = []
            for j in range(self.count):
                offsets.append(offset)
                offset = offset * self.pe[j, :, 1] + (self.rb[j, :, 0] - self.pe[j + 1, :, 0] * self.rb[j, :, 1])
            flux = jnp.zeros((self.per, ROWS, LANES), jnp.float32)
            for j in reversed(range(self.count)):
                share = (self.rt[j, :, 2] * offsets[j] + self.rb[j, :, 1]) * self.pe[j, :, 1]
                flux = flux * self.pe[j, :, 1] - share
                self.s[j, :, 0] = self.pe[j, :, 0] * flux + offsets[j]
                self.s[j, :, 1] = flux
            for target in self.others():
                self.back(self.s.at[target], self.rs.at[self.own()], part, target).start()
            self.rs[self.own()] = self.s[self.me]

        self.on_owner(body)

    def receive(self, part):
        if part >= self.parts:
            return
        low, high = self.bounds(part)

        def wait(owners):
            if owners:
                there = self.rs.at[pl.ds(0, owners * self.per)]
                self.back(there, there, part, self.others()[0]).wait_recv()

        inside = jnp.logical_and(self.me >= low, self.me < high)
        pl.when(inside)(lambda: wait(high - low - 1))
        pl.when(jnp.logical_not(inside))(lambda: wait(high - low))

    def drain(self):
        def sent(owners):
            for kind in (0, 1):
                if owners:
                    mine = self.buffers(kind)[0].at[pl.ds(0, owners * self.per)]
                    self.up(kind, mine, mine, self.others()[0]).wait_send()

        def owner():
            sent(self.owners - 1)
            mine = self.s.at[pl.ds(0, self.count - 1)]
            self.back(mine, mine, 0, self.others()[0]).wait_send()

        self.on_owner(owner)
        if self.owners < self.count:
            pl.when(jnp.logical_not(self.is_owner()))(lambda: sent(self.owners))


def kernel(nx, ny, lx, ly, nh, pitch, *refs):
    field, cond_x, cond_y, weight = refs[:4]
    out, refs = refs[4:4 + nh], refs[4 + nh - 5:]
    F, KX, KY, R, RY, HALF, HT, xh, ys, yh, ch, dl = refs[5:17]
    in_sem, halo_send, halo_recv = refs[17:20]
    x_refs, y_refs = refs[20:29], refs[29:38]
    rtx, rty = ly // ROWS, lx // ROWS
    mx, my = lax.axis_index("gx"), lax.axis_index("gy")
    X = Sweep("gx", nx, max(1, nx // 2), nh * rtx, nh, x_refs)
    Y = Sweep("gy", ny, ny, nh * rty, nh, y_refs)

    around = [(-1, 0), (1, 0), (0, -1), (0, 1), (-1, -1), (-1, 1), (1, -1), (1, 1)]

    def exists(dx, dy):
        there = None
        for d, m, n in ((dx, mx, nx), (dy, my, ny)):
            if d:
                ok = (m > 0) if d < 0 else (m < n - 1)
                there = ok if there is None else jnp.logical_and(there, ok)
        return there

    barrier = pltpu.get_barrier_semaphore()
    for target in X.others():
        pl.semaphore_signal(barrier, inc=1, device_id={"gx": target}, device_id_type=MESH)
    for target in Y.others():
        pl.semaphore_signal(barrier, inc=1, device_id={"gy": target}, device_id_type=MESH)
    for dx, dy in around[4:]:
        @pl.when(exists(dx, dy))
        def _(dx=dx, dy=dy):
            pl.semaphore_signal(barrier, inc=1, device_id={"gx": mx + dx, "gy": my + dy}, device_id_type=MESH)

    def lanes(h):
        return pl.ds(h * LANES, LANES)

    def load(k, h):
        src, dst = (
            (field, F.at[h, pl.ds(ly, lx * ly)]), (cond_x, KX.at[h]), (cond_y, KY.at[h]), (weight, R.at[h])
        )[k]
        return pltpu.make_async_copy(src.at[:, lanes(h)], dst, in_sem.at[k, h])

    def start(k):
        for h in range(nh):
            load(k, h).start()

    start(0)
    start(1)

    def halo(k):
        dx, dy = around[k]
        if dy == 0:
            src = F.at[:, pl.ds(ly if dx < 0 else lx * ly, ly), :]
            dst = xh.at[1 if dx < 0 else 0]
        elif dx == 0:
            src = ys.at[0 if dy < 0 else 1]
            dst = yh.at[1 if dy < 0 else 0]
        else:
            src = ys.at[0 if dy < 0 else 1, :, pl.ds(0 if dx < 0 else lx - ROWS, ROWS), :]
            dst = ch.at[2 * (1 if dy < 0 else 0) + (1 if dx < 0 else 0)]
        return pltpu.make_async_remote_copy(
            src_ref=src,
            dst_ref=dst,
            send_sem=halo_send.at[k],
            recv_sem=halo_recv.at[around.index((-dx, -dy))],
            device_id={"gx": mx + dx, "gy": my + dy},
            device_id_type=MESH,
        )

    def halo_in(k):
        dx, dy = around[k]
        if dy == 0:
            dst = xh.at[0 if dx < 0 else 1]
        elif dx == 0:
            dst = yh.at[0 if dy < 0 else 1]
        else:
            dst = ch.at[2 * (0 if dy < 0 else 1) + (0 if dx < 0 else 1)]
        return dst, lambda: pltpu.make_async_remote_copy(
            src_ref=dst,
            dst_ref=dst,
            send_sem=halo_send.at[k],
            recv_sem=halo_recv.at[k],
            device_id={"gx": mx + dx, "gy": my + dy},
            device_id_type=MESH,
        )

    diagonal = sum(jnp.where(exists(dx, dy), 1, 0) for dx, dy in around[4:])

    def send_halo(low, high):
        for k in range(low, high):
            @pl.when(exists(*around[k]))
            def _(k=k):
                halo(k).start()

    for h in range(nh):
        load(0, h).wait()
    start(3)
    pl.semaphore_wait(barrier, nx - 1 + ny - 1 + diagonal)
    send_halo(0, 2)
    for h in range(nh):
        ys[0, h] = F[h, pl.ds(ly, lx, stride=ly), :]
        ys[1, h] = F[h, pl.ds(ly + ly - 1, lx, stride=ly), :]
    send_halo(2, 8)

    for k, (dx, dy) in enumerate(around):
        @pl.when(jnp.logical_not(exists(dx, dy)))
        def _(k=k):
            dst = halo_in(k)[0]
            dst[...] = jnp.zeros(dst.shape, jnp.float32)

    def rows(i, n):
        return pl.ds(pl.multiple_of(i * n, n), n)

    def put_tiles(ref, h, per_plane, values):
        for c, value in enumerate(values):
            for t in range(per_plane):
                ref[h * per_plane + t, c] = value[t * ROWS:(t + 1) * ROWS]

    def get_tiles(ref, h, per_plane, c):
        return jnp.concatenate([ref[h * per_plane + t, c] for t in range(per_plane)], axis=0)

    def send_part(sweep, h):
        if sweep.parts == nh:
            sweep.send(1, h)
        elif h == nh - 1:
            sweep.send(1)

    def transfer(length, width, resistance_at):
        def steps(g, carry):
            x0, j0, x1, j1 = carry
            for r in range(ROWS):
                rho = resistance_at(g * ROWS + r)
                x0 = x0 + rho * j0
                x1 = x1 + rho * j1
                j0 = j0 + x0
                j1 = j1 + x1
            return x0, j0, x1, j1

        zero = jnp.zeros((width, LANES), jnp.float32)
        one = jnp.ones((width, LANES), jnp.float32)
        x0, j0, x1, j1 = lax.fori_loop(0, length // ROWS, steps, (one, zero, zero, one))
        return x0, x1, j0, j1

    for h in range(nh):
        load(1, h).wait()
        if h == nh - 1:
            start(2)

        def resistance_x(i, h=h):
            rho = (1.0 / step_dt) / KX[h, rows(i, ly), :]
            KX[h, rows(i, ly), :] = rho
            return rho

        put_tiles(X.t, h, rtx, transfer(lx, ly, resistance_x))
    X.send(0)

    for k, (dx, dy) in enumerate(around):
        @pl.when(exists(dx, dy))
        def _(k=k):
            halo_in(k)[1]().wait_recv()

    for h in range(nh):
        F[h, pl.ds(0, ly), :] = xh[0, h]
        F[h, pl.ds((lx + 1) * ly, ly), :] = xh[1, h]
        for side in range(2):
            edge = yh[side, h]
            before = jnp.concatenate([ch[2 * side, h, ROWS - 1:, :], edge[:-1]], axis=0)
            after = jnp.concatenate([edge[1:], ch[2 * side + 1, h, :1, :]], axis=0)
            dl[side, h] = after - before

    row = lax.broadcasted_iota(jnp.int32, (ly, LANES), 0)
    for h in range(nh):
        load(3, h).wait()

        def steps(g, carry, h=h):
            x, j = carry
            low = dl[0, h, rows(g, ROWS), :]
            high = dl[1, h, rows(g, ROWS), :]
            for r in range(ROWS):
                i = g * ROWS + r
                across = F[h, rows(i + 2, ly), :] - F[h, rows(i, ly), :]
                above = jnp.where(row == ly - 1, high[r:r + 1], pltpu.roll(across, ly - 1, 0))
                below = jnp.where(row == 0, low[r:r + 1], pltpu.roll(across, 1, 0))
                source = F[h, rows(i + 1, ly), :] + R[h, rows(i, ly), :] * (above - below) * 0.25
                R[h, rows(i, ly), :] = source
                x = x + KX[h, rows(i, ly), :] * j
                j = (j - source) + x
            return x, j

        zero = jnp.zeros((ly, LANES), jnp.float32)
        put_tiles(X.b, h, rtx, lax.fori_loop(0, lx // ROWS, steps, (zero, zero)))
        send_part(X, h)
    X.prepare()

    def transfer_y(h):
        load(2, h).wait()

        def resistance_y(i):
            rho = (1.0 / step_dt) / KY[h, pl.ds(i, lx, stride=ly), :]
            RY[h, rows(i, lx), :] = rho
            return rho

        put_tiles(Y.t, h, rty, transfer(ly, lx, resistance_y))

    for h in range(nh // 2):
        transfer_y(h)
    X.solve()
    for h in range(nh // 2, nh):
        transfer_y(h)
    Y.send(0)

    for h in range(nh):
        X.receive(h)

        def steps(g, carry, h=h):
            x, j = carry
            for r in range(ROWS):
                i = g * ROWS + r
                x = x + KX[h, rows(i, ly), :] * j
                j = (j - R[h, rows(i, ly), :]) + x
                HALF[h, pl.ds(pl.multiple_of(i * pitch, ROWS), ly), :] = x
            return x, j

        start = (get_tiles(X.rs, h, rtx, 0), get_tiles(X.rs, h, rtx, 1))
        lax.fori_loop(0, lx // ROWS, steps, start)

        def steps_y(g, carry, h=h):
            x, j = carry
            for r in range(ROWS):
                i = g * ROWS + r
                half = HALF[h, pl.ds(i, lx, stride=pitch), :]
                HT[h, rows(i, lx), :] = half
                x = x + RY[h, rows(i, lx), :] * j
                j = (j - half) + x
            return x, j

        zero = jnp.zeros((lx, LANES), jnp.float32)
        put_tiles(Y.b, h, rty, lax.fori_loop(0, ly // ROWS, steps_y, (zero, zero)))
        send_part(Y, h)

    for k, (dx, dy) in enumerate(around):
        @pl.when(exists(dx, dy))
        def _(k=k):
            halo(k).wait_send()
    X.drain()
    Y.prepare()
    Y.solve()

    for h in range(nh):
        Y.receive(h)

        def steps(g, carry, h=h):
            x, j = carry
            for r in range(ROWS):
                i = g * ROWS + r
                x = x + RY[h, rows(i, lx), :] * j
                j = (j - HT[h, rows(i, lx), :]) + x
                HALF[h, pl.ds(i, lx, stride=pitch), :] = x
            return x, j

        start = (get_tiles(Y.rs, h, rty, 0), get_tiles(Y.rs, h, rty, 1))
        lax.fori_loop(0, ly // ROWS, steps, start)

        def planes(g, carry, h=h):
            for r in range(ROWS):
                i = g * ROWS + r
                out[h][rows(i, ly), :] = HALF[h, pl.ds(pl.multiple_of(i * pitch, ROWS), ly), :]
            return carry

        lax.fori_loop(0, lx // ROWS, planes, 0)

    Y.drain()


def sweep_scratch(count, most, tiles, parts):
    per, owners = split_tiles(tiles, most)
    return [
        pltpu.VMEM((tiles, 4, ROWS, LANES), jnp.float32),
        pltpu.VMEM((count, per, 4, ROWS, LANES), jnp.float32),
        pltpu.VMEM((tiles, 2, ROWS, LANES), jnp.float32),
        pltpu.VMEM((count, per, 2, ROWS, LANES), jnp.float32),
        pltpu.VMEM((count, per, 2, ROWS, LANES), jnp.float32),
        pltpu.VMEM((tiles, 2, ROWS, LANES), jnp.float32),
        pltpu.VMEM((count + 1, per, 2, ROWS, LANES), jnp.float32),
        pltpu.SemaphoreType.DMA((2, 2)),
        pltpu.SemaphoreType.DMA((1 + parts,)),
    ]


def shards(nx, ny, field, cond_x, cond_y, cross_weight):
    lx, ly, nz = field.shape
    nh = nz // LANES
    cells = (nh, lx * ly, LANES)
    pitch = ly + ROWS if ly // ROWS % 2 == 0 else ly
    flat = [
        pltpu.with_memory_space_constraint(a.reshape(lx * ly, nz), pltpu.HBM)
        for a in (field, cond_x, cond_y, cross_weight)
    ]
    scratch = [
        pltpu.VMEM((nh, (lx + 2) * ly, LANES), jnp.float32),
        *[pltpu.VMEM(cells, jnp.float32)] * 4,
        pltpu.VMEM((nh, lx * pitch, LANES), jnp.float32),
        pltpu.VMEM(cells, jnp.float32),
        pltpu.VMEM((2, nh, ly, LANES), jnp.float32),
        pltpu.VMEM((2, nh, lx, LANES), jnp.float32),
        pltpu.VMEM((2, nh, lx, LANES), jnp.float32),
        pltpu.VMEM((4, nh, ROWS, LANES), jnp.float32),
        pltpu.VMEM((2, nh, lx, LANES), jnp.float32),
        pltpu.SemaphoreType.DMA((4, nh)),
        pltpu.SemaphoreType.DMA((8,)),
        pltpu.SemaphoreType.DMA((8,)),
        *sweep_scratch(nx, max(1, nx // 2), nh * ly // ROWS, nh),
        *sweep_scratch(ny, ny, nh * lx // ROWS, nh),
    ]
    result = pl.pallas_call(
        functools.partial(kernel, nx, ny, lx, ly, nh, pitch),
        out_shape=[pltpu.VMEM((lx * ly, LANES), jnp.float32)] * nh,
        in_specs=[pl.BlockSpec(memory_space=pltpu.HBM)] * 4,
        out_specs=[pl.BlockSpec(memory_space=pltpu.VMEM)] * nh,
        scratch_shapes=scratch,
        compiler_params=pltpu.CompilerParams(
            collective_id=0, has_side_effects=True, vmem_limit_bytes=40 * 1024 * 1024
        ),
        cost_estimate=pl.CostEstimate(
            flops=60 * lx * ly * nz, bytes_accessed=20 * lx * ly * nz, transcendentals=0
        ),
        name="adi_step",
    )(*flat)
    return jnp.concatenate(result, axis=1).reshape(lx, ly, nz)


def solution(mesh):
    spec = P("gx", "gy", None)
    return jax.shard_map(
        functools.partial(shards, mesh.shape["gx"], mesh.shape["gy"]),
        mesh=mesh,
        in_specs=(spec,) * 4,
        out_specs=spec,
        check_vma=False,
    )
```

```python
import functools
import jax
import jax.numpy as jnp
from jax import lax
from jax.sharding import PartitionSpec as P
from jax.experimental import pallas as pl
from jax.experimental.pallas import tpu as pltpu

step_dt = 16384.0
LANES = 128
ROWS = 8
MESH = pl.DeviceIdType.MESH


def split_tiles(tiles, most):
    per_owner = next(p for p in range(1, tiles + 1) if tiles % p == 0 and p * most >= tiles)
    return per_owner, tiles // per_owner


class Sweep:
    def __init__(self, axis, count, most, tiles, parts, refs):
        self.axis, self.count, self.tiles = axis, count, tiles
        self.per, self.owners = split_tiles(tiles, most)
        self.base = (count - self.owners) // 2
        self.parts = parts if self.owners % parts == 0 else 1
        (self.t, self.rt, self.b, self.rb, self.s, self.rs, self.pe, self.up_sems, self.back_sems) = refs
        self.me = lax.axis_index(axis)

    def others(self):
        return [lax.rem(self.me + d, self.count) for d in range(1, self.count)]

    def of(self, owner):
        return pl.ds((owner - self.base) * self.per, self.per)

    def own(self):
        return self.of(self.me)

    def is_owner(self):
        return jnp.logical_and(self.me >= self.base, self.me < self.base + self.owners)

    def bounds(self, part):
        each = self.owners // self.parts
        return self.base + each * part, self.base + each * (part + 1)

    def on_owner(self, body):
        if self.owners == self.count:
            body()
        else:
            pl.when(self.is_owner())(body)

    def copy(self, src, dst, send_sem, recv_sem, target):
        return pltpu.make_async_remote_copy(
            src_ref=src,
            dst_ref=dst,
            send_sem=send_sem,
            recv_sem=recv_sem,
            device_id={self.axis: target},
            device_id_type=MESH,
        )

    def buffers(self, kind):
        return ((self.t, self.rt), (self.b, self.rb))[kind]

    def up(self, kind, src, dst, target):
        return self.copy(src, dst, self.up_sems.at[kind, 0], self.up_sems.at[kind, 1], target)

    def send(self, kind, part=None):
        low, high = (self.base, self.base + self.owners) if part is None else self.bounds(part)
        mine, there = self.buffers(kind)
        for owner in range(low, high):
            @pl.when(self.me != owner)
            def _(owner=owner):
                self.up(kind, mine.at[self.of(owner)], there.at[self.me], owner).start()

            @pl.when(self.me == owner)
            def _(owner=owner):
                there[owner] = mine[self.of(owner)]

    def arrived(self, kind):
        there = self.buffers(kind)[1].at[pl.ds(0, self.count - 1)]
        self.up(kind, there, there, self.others()[0]).wait_recv()

    def prepare(self):
        def body():
            self.arrived(0)
            resistance = jnp.zeros((self.per, ROWS, LANES), jnp.float32)
            for j in range(self.count):
                inverse = 1.0 / (self.rt[j, :, 2] * resistance + self.rt[j, :, 3])
                self.pe[j, :, 0] = resistance
                self.pe[j, :, 1] = inverse
                resistance = (self.rt[j, :, 0] * resistance + self.rt[j, :, 1]) * inverse
            self.pe[self.count, :, 0] = resistance

        self.on_owner(body)

    def back(self, src, dst, part, target):
        return self.copy(src, dst, self.back_sems.at[0], self.back_sems.at[1 + part], target)

    def solve(self):
        part = lax.div(self.me - self.base, self.owners // self.parts)

        def body():
            self.arrived(1)
            offset = jnp.zeros((self.per, ROWS, LANES), jnp.float32)
            offsets = []
            for j in range(self.count):
                offsets.append(offset)
                offset = offset * self.pe[j, :, 1] + (self.rb[j, :, 0] - self.pe[j + 1, :, 0] * self.rb[j, :, 1])
            flux = jnp.zeros((self.per, ROWS, LANES), jnp.float32)
            for j in reversed(range(self.count)):
                share = (self.rt[j, :, 2] * offsets[j] + self.rb[j, :, 1]) * self.pe[j, :, 1]
                flux = flux * self.pe[j, :, 1] - share
                self.s[j, :, 0] = self.pe[j, :, 0] * flux + offsets[j]
                self.s[j, :, 1] = flux
            for target in self.others():
                self.back(self.s.at[target], self.rs.at[self.own()], part, target).start()
            self.rs[self.own()] = self.s[self.me]

        self.on_owner(body)

    def receive(self, part):
        if part >= self.parts:
            return
        low, high = self.bounds(part)

        def wait(owners):
            if owners:
                there = self.rs.at[pl.ds(0, owners * self.per)]
                self.back(there, there, part, self.others()[0]).wait_recv()

        inside = jnp.logical_and(self.me >= low, self.me < high)
        pl.when(inside)(lambda: wait(high - low - 1))
        pl.when(jnp.logical_not(inside))(lambda: wait(high - low))

    def drain(self):
        def sent(owners):
            for kind in (0, 1):
                if owners:
                    mine = self.buffers(kind)[0].at[pl.ds(0, owners * self.per)]
                    self.up(kind, mine, mine, self.others()[0]).wait_send()

        def owner():
            sent(self.owners - 1)
            mine = self.s.at[pl.ds(0, self.count - 1)]
            self.back(mine, mine, 0, self.others()[0]).wait_send()

        self.on_owner(owner)
        if self.owners < self.count:
            pl.when(jnp.logical_not(self.is_owner()))(lambda: sent(self.owners))


class Gathered:
    def __init__(self, axis, count, tiles, parts, refs):
        self.axis, self.count, self.parts = axis, count, parts
        self.tiles = tiles // parts
        (self.t, self.rt, self.b, self.rb, self.s, self.pe, self.send_sems, self.recv_sems) = refs
        self.me = lax.axis_index(axis)

    def others(self):
        return [lax.rem(self.me + d, self.count) for d in range(1, self.count)]

    def copy(self, src, dst, send, recv, target):
        return pltpu.make_async_remote_copy(
            src_ref=src,
            dst_ref=dst,
            send_sem=self.send_sems.at[send],
            recv_sem=self.recv_sems.at[recv],
            device_id={self.axis: target},
            device_id_type=MESH,
        )

    def send_matrices(self):
        for target in self.others():
            self.copy(self.t, self.rt.at[self.me], 0, 0, target).start()
        self.rt[self.me] = self.t[...]

    def send(self, part):
        for target in self.others():
            self.copy(self.b.at[part], self.rb.at[part, self.me], 1, 1 + part, target).start()
        self.rb[part, self.me] = self.b[part]

    def prepare(self):
        there = self.rt.at[pl.ds(0, self.count - 1)]
        self.copy(there, there, 0, 0, self.others()[0]).wait_recv()
        for part in range(self.parts):
            resistance = jnp.zeros((self.tiles, ROWS, LANES), jnp.float32)
            for j in range(self.count):
                through, shunt, last = (self.rt[j, part, :, c] for c in range(3))
                inverse = 1.0 / (shunt * resistance + last)
                self.pe[j, part, 0] = resistance
                self.pe[j, part, 1] = inverse
                resistance = (resistance * inverse + through) / last
            self.pe[self.count, part, 0] = resistance

    def solve(self, part):
        there = self.rb.at[part, pl.ds(0, self.count - 1)]
        self.copy(there, there, 1, 1 + part, self.others()[0]).wait_recv()
        offset = jnp.zeros((self.tiles, ROWS, LANES), jnp.float32)
        offsets = []
        for j in range(self.count):
            offsets.append(offset)
            value, flux = self.rb[part, j, :, 0], self.rb[part, j, :, 1]
            offset = offset * self.pe[j, part, 1] + (value - self.pe[j + 1, part, 0] * flux)
        flux = jnp.zeros((self.tiles, ROWS, LANES), jnp.float32)
        for j in reversed(range(self.count)):
            share = self.rt[j, part, :, 1] * offsets[j] + self.rb[part, j, :, 1]
            flux = (flux - share) * self.pe[j, part, 1]
            self.s[j, 0] = self.pe[j, part, 0] * flux + offsets[j]
            self.s[j, 1] = flux
        state = self.s[self.me]
        return [state[c].reshape(self.tiles * ROWS, LANES) for c in range(2)]

    def drain(self):
        mine = self.rt.at[pl.ds(0, self.count - 1)]
        self.copy(mine, mine, 0, 0, self.others()[0]).wait_send()
        mine = self.rb.at[:, pl.ds(0, self.count - 1)]
        self.copy(mine, mine, 1, 1, self.others()[0]).wait_send()


def kernel(nx, ny, lx, ly, nh, pitch, *refs):
    field, cond_x, cond_y, weight = refs[:4]
    out, refs = refs[4:4 + nh], refs[4 + nh - 5:]
    F, KX, KY, R, RY, HALF, HT, xh, ys, yh, ch, dl = refs[5:17]
    in_sem, halo_send, halo_recv = refs[17:20]
    x_refs, y_refs = refs[20:29], refs[29:37]
    rtx, rty = ly // ROWS, lx // ROWS
    mx, my = lax.axis_index("gx"), lax.axis_index("gy")
    X = Sweep("gx", nx, max(1, nx // 2), nh * rtx, nh, x_refs)
    Y = Gathered("gy", ny, nh * rty, nh, y_refs)

    around = [(-1, 0), (1, 0), (0, -1), (0, 1), (-1, -1), (-1, 1), (1, -1), (1, 1)]

    def exists(dx, dy):
        there = None
        for d, m, n in ((dx, mx, nx), (dy, my, ny)):
            if d:
                ok = (m > 0) if d < 0 else (m < n - 1)
                there = ok if there is None else jnp.logical_and(there, ok)
        return there

    barrier = pltpu.get_barrier_semaphore()
    for target in X.others():
        pl.semaphore_signal(barrier, inc=1, device_id={"gx": target}, device_id_type=MESH)
    for target in Y.others():
        pl.semaphore_signal(barrier, inc=1, device_id={"gy": target}, device_id_type=MESH)
    for dx, dy in around[4:]:
        @pl.when(exists(dx, dy))
        def _(dx=dx, dy=dy):
            pl.semaphore_signal(barrier, inc=1, device_id={"gx": mx + dx, "gy": my + dy}, device_id_type=MESH)

    def lanes(h):
        return pl.ds(h * LANES, LANES)

    def load(k, h):
        src, dst = (
            (field, F.at[h, pl.ds(ly, lx * ly)]), (cond_x, KX.at[h]), (cond_y, KY.at[h]), (weight, R.at[h])
        )[k]
        return pltpu.make_async_copy(src.at[:, lanes(h)], dst, in_sem.at[k, h])

    def start(k):
        for h in range(nh):
            load(k, h).start()

    start(0)
    start(1)

    def halo(k):
        dx, dy = around[k]
        if dy == 0:
            src = F.at[:, pl.ds(ly if dx < 0 else lx * ly, ly), :]
            dst = xh.at[1 if dx < 0 else 0]
        elif dx == 0:
            src = ys.at[0 if dy < 0 else 1]
            dst = yh.at[1 if dy < 0 else 0]
        else:
            src = ys.at[0 if dy < 0 else 1, :, pl.ds(0 if dx < 0 else lx - ROWS, ROWS), :]
            dst = ch.at[2 * (1 if dy < 0 else 0) + (1 if dx < 0 else 0)]
        return pltpu.make_async_remote_copy(
            src_ref=src,
            dst_ref=dst,
            send_sem=halo_send.at[k],
            recv_sem=halo_recv.at[around.index((-dx, -dy))],
            device_id={"gx": mx + dx, "gy": my + dy},
            device_id_type=MESH,
        )

    def halo_in(k):
        dx, dy = around[k]
        if dy == 0:
            dst = xh.at[0 if dx < 0 else 1]
        elif dx == 0:
            dst = yh.at[0 if dy < 0 else 1]
        else:
            dst = ch.at[2 * (0 if dy < 0 else 1) + (0 if dx < 0 else 1)]
        return dst, lambda: pltpu.make_async_remote_copy(
            src_ref=dst,
            dst_ref=dst,
            send_sem=halo_send.at[k],
            recv_sem=halo_recv.at[k],
            device_id={"gx": mx + dx, "gy": my + dy},
            device_id_type=MESH,
        )

    diagonal = sum(jnp.where(exists(dx, dy), 1, 0) for dx, dy in around[4:])

    def send_halo(low, high):
        for k in range(low, high):
            @pl.when(exists(*around[k]))
            def _(k=k):
                halo(k).start()

    for h in range(nh):
        load(0, h).wait()
    start(3)
    pl.semaphore_wait(barrier, nx - 1 + ny - 1 + diagonal)
    send_halo(0, 2)
    for h in range(nh):
        ys[0, h] = F[h, pl.ds(ly, lx, stride=ly), :]
        ys[1, h] = F[h, pl.ds(ly + ly - 1, lx, stride=ly), :]
    send_halo(2, 8)

    for k, (dx, dy) in enumerate(around):
        @pl.when(jnp.logical_not(exists(dx, dy)))
        def _(k=k):
            dst = halo_in(k)[0]
            dst[...] = jnp.zeros(dst.shape, jnp.float32)

    def rows(i, n):
        return pl.ds(pl.multiple_of(i * n, n), n)

    def put_tiles(ref, h, per_plane, values):
        for c, value in enumerate(values):
            for t in range(per_plane):
                ref[h * per_plane + t, c] = value[t * ROWS:(t + 1) * ROWS]

    def get_tiles(ref, h, per_plane, c):
        return jnp.concatenate([ref[h * per_plane + t, c] for t in range(per_plane)], axis=0)

    def send_part(sweep, h):
        if sweep.parts == nh:
            sweep.send(1, h)
        elif h == nh - 1:
            sweep.send(1)

    def transfer(length, width, resistance_at):
        def steps(g, carry):
            x0, j0, x1, j1 = carry
            for r in range(ROWS):
                rho = resistance_at(g * ROWS + r)
                x0 = x0 + rho * j0
                x1 = x1 + rho * j1
                j0 = j0 + x0
                j1 = j1 + x1
            return x0, j0, x1, j1

        zero = jnp.zeros((width, LANES), jnp.float32)
        one = jnp.ones((width, LANES), jnp.float32)
        x0, j0, x1, j1 = lax.fori_loop(0, length // ROWS, steps, (one, zero, zero, one))
        return x0, x1, j0, j1

    for h in range(nh):
        load(1, h).wait()
        if h == nh - 1:
            start(2)

        def resistance_x(i, h=h):
            rho = (1.0 / step_dt) / KX[h, rows(i, ly), :]
            KX[h, rows(i, ly), :] = rho
            return rho

        put_tiles(X.t, h, rtx, transfer(lx, ly, resistance_x))
    X.send(0)

    for k, (dx, dy) in enumerate(around):
        @pl.when(exists(dx, dy))
        def _(k=k):
            halo_in(k)[1]().wait_recv()

    for h in range(nh):
        F[h, pl.ds(0, ly), :] = xh[0, h]
        F[h, pl.ds((lx + 1) * ly, ly), :] = xh[1, h]
        for side in range(2):
            edge = yh[side, h]
            before = jnp.concatenate([ch[2 * side, h, ROWS - 1:, :], edge[:-1]], axis=0)
            after = jnp.concatenate([edge[1:], ch[2 * side + 1, h, :1, :]], axis=0)
            dl[side, h] = after - before

    row = lax.broadcasted_iota(jnp.int32, (ly, LANES), 0)
    for h in range(nh):
        load(3, h).wait()

        def steps(g, carry, h=h):
            x, j = carry
            low = dl[0, h, rows(g, ROWS), :]
            high = dl[1, h, rows(g, ROWS), :]
            for r in range(ROWS):
                i = g * ROWS + r
                across = F[h, rows(i + 2, ly), :] - F[h, rows(i, ly), :]
                above = jnp.where(row == ly - 1, high[r:r + 1], pltpu.roll(across, ly - 1, 0))
                below = jnp.where(row == 0, low[r:r + 1], pltpu.roll(across, 1, 0))
                source = F[h, rows(i + 1, ly), :] + R[h, rows(i, ly), :] * (above - below) * 0.25
                R[h, rows(i, ly), :] = source
                x = x + KX[h, rows(i, ly), :] * j
                j = (j - source) + x
            return x, j

        zero = jnp.zeros((ly, LANES), jnp.float32)
        put_tiles(X.b, h, rtx, lax.fori_loop(0, lx // ROWS, steps, (zero, zero)))
        send_part(X, h)
    X.prepare()

    def transfer_y(h):
        load(2, h).wait()

        def resistance_y(i):
            rho = (1.0 / step_dt) / KY[h, pl.ds(i, lx, stride=ly), :]
            RY[h, rows(i, lx), :] = rho
            return rho

        _, through, shunt, last = transfer(ly, lx, resistance_y)
        put_tiles(Y.t.at[h], 0, rty, (through, shunt, last))

    for h in range(nh // 2):
        transfer_y(h)
    X.solve()
    for h in range(nh // 2, nh):
        transfer_y(h)
    Y.send_matrices()

    for h in range(nh):
        X.receive(h)

        def steps(g, carry, h=h):
            x, j = carry
            for r in range(ROWS):
                i = g * ROWS + r
                x = x + KX[h, rows(i, ly), :] * j
                j = (j - R[h, rows(i, ly), :]) + x
                HALF[h, pl.ds(pl.multiple_of(i * pitch, ROWS), ly), :] = x
            return x, j

        start = (get_tiles(X.rs, h, rtx, 0), get_tiles(X.rs, h, rtx, 1))
        lax.fori_loop(0, lx // ROWS, steps, start)

        def steps_y(g, carry, h=h):
            x, j = carry
            for r in range(ROWS):
                i = g * ROWS + r
                half = HALF[h, pl.ds(i, lx, stride=pitch), :]
                HT[h, rows(i, lx), :] = half
                x = x + RY[h, rows(i, lx), :] * j
                j = (j - half) + x
            return x, j

        zero = jnp.zeros((lx, LANES), jnp.float32)
        put_tiles(Y.b.at[h], 0, rty, lax.fori_loop(0, ly // ROWS, steps_y, (zero, zero)))
        Y.send(h)

    for k, (dx, dy) in enumerate(around):
        @pl.when(exists(dx, dy))
        def _(k=k):
            halo(k).wait_send()
    X.drain()
    Y.prepare()

    for h in range(nh):
        start = Y.solve(h)

        def steps(g, carry, h=h):
            x, j = carry
            for r in range(ROWS):
                i = g * ROWS + r
                x = x + RY[h, rows(i, lx), :] * j
                j = (j - HT[h, rows(i, lx), :]) + x
                HALF[h, pl.ds(i, lx, stride=pitch), :] = x
            return x, j

        lax.fori_loop(0, ly // ROWS, steps, tuple(start))

        def planes(g, carry, h=h):
            for r in range(ROWS):
                i = g * ROWS + r
                out[h][rows(i, ly), :] = HALF[h, pl.ds(pl.multiple_of(i * pitch, ROWS), ly), :]
            return carry

        lax.fori_loop(0, lx // ROWS, planes, 0)

    Y.drain()


def sweep_scratch(count, most, tiles, parts):
    per, owners = split_tiles(tiles, most)
    return [
        pltpu.VMEM((tiles, 4, ROWS, LANES), jnp.float32),
        pltpu.VMEM((count, per, 4, ROWS, LANES), jnp.float32),
        pltpu.VMEM((tiles, 2, ROWS, LANES), jnp.float32),
        pltpu.VMEM((count, per, 2, ROWS, LANES), jnp.float32),
        pltpu.VMEM((count, per, 2, ROWS, LANES), jnp.float32),
        pltpu.VMEM((tiles, 2, ROWS, LANES), jnp.float32),
        pltpu.VMEM((count + 1, per, 2, ROWS, LANES), jnp.float32),
        pltpu.SemaphoreType.DMA((2, 2)),
        pltpu.SemaphoreType.DMA((1 + parts,)),
    ]


def gathered_scratch(count, tiles, parts):
    each = tiles // parts
    return [
        pltpu.VMEM((parts, each, 3, ROWS, LANES), jnp.float32),
        pltpu.VMEM((count, parts, each, 3, ROWS, LANES), jnp.float32),
        pltpu.VMEM((parts, each, 2, ROWS, LANES), jnp.float32),
        pltpu.VMEM((parts, count, each, 2, ROWS, LANES), jnp.float32),
        pltpu.VMEM((count, 2, each, ROWS, LANES), jnp.float32),
        pltpu.VMEM((count + 1, parts, 2, each, ROWS, LANES), jnp.float32),
        pltpu.SemaphoreType.DMA((2,)),
        pltpu.SemaphoreType.DMA((1 + parts,)),
    ]


def shards(nx, ny, field, cond_x, cond_y, cross_weight):
    lx, ly, nz = field.shape
    nh = nz // LANES
    cells = (nh, lx * ly, LANES)
    pitch = ly + ROWS if ly // ROWS % 2 == 0 else ly
    flat = [
        pltpu.with_memory_space_constraint(a.reshape(lx * ly, nz), pltpu.HBM)
        for a in (field, cond_x, cond_y, cross_weight)
    ]
    scratch = [
        pltpu.VMEM((nh, (lx + 2) * ly, LANES), jnp.float32),
        *[pltpu.VMEM(cells, jnp.float32)] * 4,
        pltpu.VMEM((nh, lx * pitch, LANES), jnp.float32),
        pltpu.VMEM(cells, jnp.float32),
        pltpu.VMEM((2, nh, ly, LANES), jnp.float32),
        pltpu.VMEM((2, nh, lx, LANES), jnp.float32),
        pltpu.VMEM((2, nh, lx, LANES), jnp.float32),
        pltpu.VMEM((4, nh, ROWS, LANES), jnp.float32),
        pltpu.VMEM((2, nh, lx, LANES), jnp.float32),
        pltpu.SemaphoreType.DMA((4, nh)),
        pltpu.SemaphoreType.DMA((8,)),
        pltpu.SemaphoreType.DMA((8,)),
        *sweep_scratch(nx, max(1, nx // 2), nh * ly // ROWS, nh),
        *gathered_scratch(ny, nh * lx // ROWS, nh),
    ]
    result = pl.pallas_call(
        functools.partial(kernel, nx, ny, lx, ly, nh, pitch),
        out_shape=[pltpu.VMEM((lx * ly, LANES), jnp.float32)] * nh,
        in_specs=[pl.BlockSpec(memory_space=pltpu.HBM)] * 4,
        out_specs=[pl.BlockSpec(memory_space=pltpu.VMEM)] * nh,
        scratch_shapes=scratch,
        compiler_params=pltpu.CompilerParams(
            collective_id=0, has_side_effects=True, vmem_limit_bytes=40 * 1024 * 1024
        ),
        cost_estimate=pl.CostEstimate(
            flops=60 * lx * ly * nz, bytes_accessed=20 * lx * ly * nz, transcendentals=0
        ),
        name="adi_step",
    )(*flat)
    return jnp.concatenate(result, axis=1).reshape(lx, ly, nz)


def solution(mesh):
    spec = P("gx", "gy", None)
    return jax.shard_map(
        functools.partial(shards, mesh.shape["gx"], mesh.shape["gy"]),
        mesh=mesh,
        in_specs=(spec,) * 4,
        out_specs=spec,
        check_vma=False,
    )
```

```python
import functools
import jax
import jax.numpy as jnp
from jax import lax
from jax.sharding import PartitionSpec as P
from jax.experimental import pallas as pl
from jax.experimental.pallas import tpu as pltpu

step_dt = 16384.0
LANES = 128
ROWS = 8
MESH = pl.DeviceIdType.MESH


def split_tiles(tiles, most):
    per_owner = next(p for p in range(1, tiles + 1) if tiles % p == 0 and p * most >= tiles)
    return per_owner, tiles // per_owner


class Sweep:
    def __init__(self, axis, count, most, tiles, parts, refs):
        self.axis, self.count, self.tiles = axis, count, tiles
        self.per, self.owners = split_tiles(tiles, most)
        self.base = (count - self.owners) // 2
        self.parts = parts if self.owners % parts == 0 else 1
        (self.t, self.rt, self.b, self.rb, self.s, self.rs, self.pe, self.up_sems, self.back_sems) = refs
        self.me = lax.axis_index(axis)

    def others(self):
        return [lax.rem(self.me + d, self.count) for d in range(1, self.count)]

    def of(self, owner):
        return pl.ds((owner - self.base) * self.per, self.per)

    def own(self):
        return self.of(self.me)

    def is_owner(self):
        return jnp.logical_and(self.me >= self.base, self.me < self.base + self.owners)

    def bounds(self, part):
        each = self.owners // self.parts
        return self.base + each * part, self.base + each * (part + 1)

    def on_owner(self, body):
        if self.owners == self.count:
            body()
        else:
            pl.when(self.is_owner())(body)

    def copy(self, src, dst, send_sem, recv_sem, target):
        return pltpu.make_async_remote_copy(
            src_ref=src,
            dst_ref=dst,
            send_sem=send_sem,
            recv_sem=recv_sem,
            device_id={self.axis: target},
            device_id_type=MESH,
        )

    def buffers(self, kind):
        return ((self.t, self.rt), (self.b, self.rb))[kind]

    def up(self, kind, src, dst, target):
        return self.copy(src, dst, self.up_sems.at[kind, 0], self.up_sems.at[kind, 1], target)

    def send(self, kind, part=None):
        low, high = (self.base, self.base + self.owners) if part is None else self.bounds(part)
        mine, there = self.buffers(kind)
        for owner in range(low, high):
            @pl.when(self.me != owner)
            def _(owner=owner):
                self.up(kind, mine.at[self.of(owner)], there.at[self.me], owner).start()

            @pl.when(self.me == owner)
            def _(owner=owner):
                there[owner] = mine[self.of(owner)]

    def arrived(self, kind):
        there = self.buffers(kind)[1].at[pl.ds(0, self.count - 1)]
        self.up(kind, there, there, self.others()[0]).wait_recv()

    def prepare(self):
        def body():
            self.arrived(0)
            resistance = jnp.zeros((self.per, ROWS, LANES), jnp.float32)
            for j in range(self.count):
                inverse = 1.0 / (self.rt[j, :, 2] * resistance + self.rt[j, :, 3])
                self.pe[j, :, 0] = resistance
                self.pe[j, :, 1] = inverse
                resistance = (self.rt[j, :, 0] * resistance + self.rt[j, :, 1]) * inverse
            self.pe[self.count, :, 0] = resistance

        self.on_owner(body)

    def back(self, src, dst, part, target):
        return self.copy(src, dst, self.back_sems.at[0], self.back_sems.at[1 + part], target)

    def solve(self):
        part = lax.div(self.me - self.base, self.owners // self.parts)

        def body():
            self.arrived(1)
            offset = jnp.zeros((self.per, ROWS, LANES), jnp.float32)
            offsets = []
            for j in range(self.count):
                offsets.append(offset)
                offset = offset * self.pe[j, :, 1] + (self.rb[j, :, 0] - self.pe[j + 1, :, 0] * self.rb[j, :, 1])
            flux = jnp.zeros((self.per, ROWS, LANES), jnp.float32)
            for j in reversed(range(self.count)):
                share = (self.rt[j, :, 2] * offsets[j] + self.rb[j, :, 1]) * self.pe[j, :, 1]
                flux = flux * self.pe[j, :, 1] - share
                self.s[j, :, 0] = self.pe[j, :, 0] * flux + offsets[j]
                self.s[j, :, 1] = flux
            for target in self.others():
                self.back(self.s.at[target], self.rs.at[self.own()], part, target).start()
            self.rs[self.own()] = self.s[self.me]

        self.on_owner(body)

    def receive(self, part):
        if part >= self.parts:
            return
        low, high = self.bounds(part)

        def wait(owners):
            if owners:
                there = self.rs.at[pl.ds(0, owners * self.per)]
                self.back(there, there, part, self.others()[0]).wait_recv()

        inside = jnp.logical_and(self.me >= low, self.me < high)
        pl.when(inside)(lambda: wait(high - low - 1))
        pl.when(jnp.logical_not(inside))(lambda: wait(high - low))

    def drain(self):
        def sent(owners):
            for kind in (0, 1):
                if owners:
                    mine = self.buffers(kind)[0].at[pl.ds(0, owners * self.per)]
                    self.up(kind, mine, mine, self.others()[0]).wait_send()

        def owner():
            sent(self.owners - 1)
            mine = self.s.at[pl.ds(0, self.count - 1)]
            self.back(mine, mine, 0, self.others()[0]).wait_send()

        self.on_owner(owner)
        if self.owners < self.count:
            pl.when(jnp.logical_not(self.is_owner()))(lambda: sent(self.owners))


class Gathered:
    def __init__(self, axis, count, tiles, parts, refs):
        self.axis, self.count, self.parts = axis, count, parts
        self.tiles = tiles // parts
        (self.t, self.rt, self.b, self.rb, self.w, self.pe, self.send_sems, self.recv_sems) = refs
        self.me = lax.axis_index(axis)

    def others(self):
        return [lax.rem(self.me + d, self.count) for d in range(1, self.count)]

    def copy(self, src, dst, send, recv, target):
        return pltpu.make_async_remote_copy(
            src_ref=src,
            dst_ref=dst,
            send_sem=self.send_sems.at[send],
            recv_sem=self.recv_sems.at[recv],
            device_id={self.axis: target},
            device_id_type=MESH,
        )

    def send_matrices(self, part):
        for target in self.others():
            self.copy(self.t.at[part], self.rt.at[part, self.me], 0, part, target).start()
        self.rt[part, self.me] = self.t[part]

    def prepare(self, part):
        there = self.rt.at[part, pl.ds(0, self.count - 1)]
        self.copy(there, there, 0, part, self.others()[0]).wait_recv()
        low = jnp.zeros((self.tiles, ROWS, LANES), jnp.float32)
        for j in range(self.count):
            through, shunt, last = (self.rt[part, j, :, c] for c in range(3))
            inverse = 1.0 / (shunt * low + last)
            self.pe[part, j, 0] = low
            self.pe[part, j, 1] = inverse
            low = (low * inverse + through) / last
        self.pe[part, self.count, 0] = low
        high = jnp.zeros((self.tiles, ROWS, LANES), jnp.float32)
        for j in reversed(range(self.count)):
            through, shunt, last = (self.rt[part, j, :, c] for c in range(3))
            inverse = 1.0 / (last + high * through)
            self.pe[part, j + 1, 2] = high
            self.pe[part, j, 3] = inverse
            high = (high * inverse + shunt) / last
        self.pe[part, 0, 2] = high

    def send(self, part):
        value, flux = self.b[part, :, 0], self.b[part, :, 1]
        self.w[part, 0] = value - self.pe[part, self.me + 1, 0] * flux
        self.w[part, 1] = flux + self.pe[part, self.me + 1, 2] * value
        for target in self.others():
            side = jnp.where(target > self.me, 0, 1)
            self.copy(self.w.at[part, side], self.rb.at[part, self.me], 1, self.parts + part, target).start()
        self.rb[part, self.me] = self.w[part, 1]

    def solve(self, part):
        there = self.rb.at[part, pl.ds(0, self.count - 1)]
        self.copy(there, there, 1, self.parts + part, self.others()[0]).wait_recv()
        offset = jnp.zeros((self.tiles, ROWS, LANES), jnp.float32)
        for j in range(self.count - 1):
            offset = jnp.where(j < self.me, offset * self.pe[part, j, 1] + self.rb[part, j], offset)
        push = jnp.zeros((self.tiles, ROWS, LANES), jnp.float32)
        for j in reversed(range(self.count)):
            push = jnp.where(j >= self.me, (push - self.rb[part, j]) * self.pe[part, j, 3], push)
        low, high = self.pe[part, self.me, 0], self.pe[part, self.me, 2]
        flux = (push - high * offset) / (1.0 + high * low)
        state = (low * flux + offset, flux)
        return [value.reshape(self.tiles * ROWS, LANES) for value in state]

    def drain(self):
        mine = self.rt.at[:, pl.ds(0, self.count - 1)]
        self.copy(mine, mine, 0, 0, self.others()[0]).wait_send()
        mine = self.rb.at[:, pl.ds(0, self.count - 1)]
        self.copy(mine, mine, 1, 1, self.others()[0]).wait_send()


def kernel(nx, ny, lx, ly, nh, pitch, *refs):
    field, cond_x, cond_y, weight = refs[:4]
    out, refs = refs[4:4 + nh], refs[4 + nh - 5:]
    F, KX, KY, R, RY, HALF, HT, xh, ys, yh, ch, dl = refs[5:17]
    in_sem, halo_send, halo_recv = refs[17:20]
    x_refs, y_refs = refs[20:29], refs[29:37]
    rtx, rty = ly // ROWS, lx // ROWS
    mx, my = lax.axis_index("gx"), lax.axis_index("gy")
    X = Sweep("gx", nx, max(1, nx // 2), nh * rtx, nh, x_refs)
    Y = Gathered("gy", ny, nh * rty, nh, y_refs)

    around = [(-1, 0), (1, 0), (0, -1), (0, 1), (-1, -1), (-1, 1), (1, -1), (1, 1)]

    def exists(dx, dy):
        there = None
        for d, m, n in ((dx, mx, nx), (dy, my, ny)):
            if d:
                ok = (m > 0) if d < 0 else (m < n - 1)
                there = ok if there is None else jnp.logical_and(there, ok)
        return there

    barrier = pltpu.get_barrier_semaphore()
    for target in X.others():
        pl.semaphore_signal(barrier, inc=1, device_id={"gx": target}, device_id_type=MESH)
    for target in Y.others():
        pl.semaphore_signal(barrier, inc=1, device_id={"gy": target}, device_id_type=MESH)
    for dx, dy in around[4:]:
        @pl.when(exists(dx, dy))
        def _(dx=dx, dy=dy):
            pl.semaphore_signal(barrier, inc=1, device_id={"gx": mx + dx, "gy": my + dy}, device_id_type=MESH)

    def lanes(h):
        return pl.ds(h * LANES, LANES)

    def load(k, h):
        src, dst = (
            (field, F.at[h, pl.ds(ly, lx * ly)]), (cond_x, KX.at[h]), (cond_y, KY.at[h]), (weight, R.at[h])
        )[k]
        return pltpu.make_async_copy(src.at[:, lanes(h)], dst, in_sem.at[k, h])

    def start(k):
        for h in range(nh):
            load(k, h).start()

    start(0)
    start(1)

    def halo(k):
        dx, dy = around[k]
        if dy == 0:
            src = F.at[:, pl.ds(ly if dx < 0 else lx * ly, ly), :]
            dst = xh.at[1 if dx < 0 else 0]
        elif dx == 0:
            src = ys.at[0 if dy < 0 else 1]
            dst = yh.at[1 if dy < 0 else 0]
        else:
            src = ys.at[0 if dy < 0 else 1, :, pl.ds(0 if dx < 0 else lx - ROWS, ROWS), :]
            dst = ch.at[2 * (1 if dy < 0 else 0) + (1 if dx < 0 else 0)]
        return pltpu.make_async_remote_copy(
            src_ref=src,
            dst_ref=dst,
            send_sem=halo_send.at[k],
            recv_sem=halo_recv.at[around.index((-dx, -dy))],
            device_id={"gx": mx + dx, "gy": my + dy},
            device_id_type=MESH,
        )

    def halo_in(k):
        dx, dy = around[k]
        if dy == 0:
            dst = xh.at[0 if dx < 0 else 1]
        elif dx == 0:
            dst = yh.at[0 if dy < 0 else 1]
        else:
            dst = ch.at[2 * (0 if dy < 0 else 1) + (0 if dx < 0 else 1)]
        return dst, lambda: pltpu.make_async_remote_copy(
            src_ref=dst,
            dst_ref=dst,
            send_sem=halo_send.at[k],
            recv_sem=halo_recv.at[k],
            device_id={"gx": mx + dx, "gy": my + dy},
            device_id_type=MESH,
        )

    diagonal = sum(jnp.where(exists(dx, dy), 1, 0) for dx, dy in around[4:])

    def send_halo(low, high):
        for k in range(low, high):
            @pl.when(exists(*around[k]))
            def _(k=k):
                halo(k).start()

    for h in range(nh):
        load(0, h).wait()
    start(3)
    pl.semaphore_wait(barrier, nx - 1 + ny - 1 + diagonal)
    send_halo(0, 2)
    for h in range(nh):
        ys[0, h] = F[h, pl.ds(ly, lx, stride=ly), :]
        ys[1, h] = F[h, pl.ds(ly + ly - 1, lx, stride=ly), :]
    send_halo(2, 8)

    for k, (dx, dy) in enumerate(around):
        @pl.when(jnp.logical_not(exists(dx, dy)))
        def _(k=k):
            dst = halo_in(k)[0]
            dst[...] = jnp.zeros(dst.shape, jnp.float32)

    def rows(i, n):
        return pl.ds(pl.multiple_of(i * n, n), n)

    def put_tiles(ref, h, per_plane, values):
        for c, value in enumerate(values):
            for t in range(per_plane):
                ref[h * per_plane + t, c] = value[t * ROWS:(t + 1) * ROWS]

    def get_tiles(ref, h, per_plane, c):
        return jnp.concatenate([ref[h * per_plane + t, c] for t in range(per_plane)], axis=0)

    def send_part(sweep, h):
        if sweep.parts == nh:
            sweep.send(1, h)
        elif h == nh - 1:
            sweep.send(1)

    def transfer(length, width, resistance_at):
        def steps(g, carry):
            x0, j0, x1, j1 = carry
            for r in range(ROWS):
                rho = resistance_at(g * ROWS + r)
                x0 = x0 + rho * j0
                x1 = x1 + rho * j1
                j0 = j0 + x0
                j1 = j1 + x1
            return x0, j0, x1, j1

        zero = jnp.zeros((width, LANES), jnp.float32)
        one = jnp.ones((width, LANES), jnp.float32)
        x0, j0, x1, j1 = lax.fori_loop(0, length // ROWS, steps, (one, zero, zero, one))
        return x0, x1, j0, j1

    for h in range(nh):
        load(1, h).wait()
        if h == nh - 1:
            start(2)

        def resistance_x(i, h=h):
            rho = (1.0 / step_dt) / KX[h, rows(i, ly), :]
            KX[h, rows(i, ly), :] = rho
            return rho

        put_tiles(X.t, h, rtx, transfer(lx, ly, resistance_x))
    X.send(0)

    for k, (dx, dy) in enumerate(around):
        @pl.when(exists(dx, dy))
        def _(k=k):
            halo_in(k)[1]().wait_recv()

    for h in range(nh):
        F[h, pl.ds(0, ly), :] = xh[0, h]
        F[h, pl.ds((lx + 1) * ly, ly), :] = xh[1, h]
        for side in range(2):
            edge = yh[side, h]
            before = jnp.concatenate([ch[2 * side, h, ROWS - 1:, :], edge[:-1]], axis=0)
            after = jnp.concatenate([edge[1:], ch[2 * side + 1, h, :1, :]], axis=0)
            dl[side, h] = after - before

    row = lax.broadcasted_iota(jnp.int32, (ly, LANES), 0)
    for h in range(nh):
        load(3, h).wait()

        def steps(g, carry, h=h):
            x, j = carry
            low = dl[0, h, rows(g, ROWS), :]
            high = dl[1, h, rows(g, ROWS), :]
            for r in range(ROWS):
                i = g * ROWS + r
                across = F[h, rows(i + 2, ly), :] - F[h, rows(i, ly), :]
                above = jnp.where(row == ly - 1, high[r:r + 1], pltpu.roll(across, ly - 1, 0))
                below = jnp.where(row == 0, low[r:r + 1], pltpu.roll(across, 1, 0))
                source = F[h, rows(i + 1, ly), :] + R[h, rows(i, ly), :] * (above - below) * 0.25
                R[h, rows(i, ly), :] = source
                x = x + KX[h, rows(i, ly), :] * j
                j = (j - source) + x
            return x, j

        zero = jnp.zeros((ly, LANES), jnp.float32)
        put_tiles(X.b, h, rtx, lax.fori_loop(0, lx // ROWS, steps, (zero, zero)))
        send_part(X, h)
    X.prepare()

    def transfer_y(h):
        load(2, h).wait()

        def resistance_y(i):
            rho = (1.0 / step_dt) / KY[h, pl.ds(i, lx, stride=ly), :]
            RY[h, rows(i, lx), :] = rho
            return rho

        _, through, shunt, last = transfer(ly, lx, resistance_y)
        put_tiles(Y.t.at[h], 0, rty, (through, shunt, last))

    for h in range(nh):
        transfer_y(h)
        Y.send_matrices(h)
    X.solve()

    for h in range(nh):
        Y.prepare(h)
        X.receive(h)

        def steps(g, carry, h=h):
            x, j = carry
            for r in range(ROWS):
                i = g * ROWS + r
                x = x + KX[h, rows(i, ly), :] * j
                j = (j - R[h, rows(i, ly), :]) + x
                HALF[h, pl.ds(pl.multiple_of(i * pitch, ROWS), ly), :] = x
            return x, j

        start = (get_tiles(X.rs, h, rtx, 0), get_tiles(X.rs, h, rtx, 1))
        lax.fori_loop(0, lx // ROWS, steps, start)

        def steps_y(g, carry, h=h):
            x, j = carry
            for r in range(ROWS):
                i = g * ROWS + r
                half = HALF[h, pl.ds(i, lx, stride=pitch), :]
                HT[h, rows(i, lx), :] = half
                x = x + RY[h, rows(i, lx), :] * j
                j = (j - half) + x
            return x, j

        zero = jnp.zeros((lx, LANES), jnp.float32)
        put_tiles(Y.b.at[h], 0, rty, lax.fori_loop(0, ly // ROWS, steps_y, (zero, zero)))
        Y.send(h)

    for k, (dx, dy) in enumerate(around):
        @pl.when(exists(dx, dy))
        def _(k=k):
            halo(k).wait_send()
    X.drain()

    for h in range(nh):
        start = Y.solve(h)

        def steps(g, carry, h=h):
            x, j = carry
            for r in range(ROWS):
                i = g * ROWS + r
                x = x + RY[h, rows(i, lx), :] * j
                j = (j - HT[h, rows(i, lx), :]) + x
                HALF[h, pl.ds(i, lx, stride=pitch), :] = x
            return x, j

        lax.fori_loop(0, ly // ROWS, steps, tuple(start))

        def planes(g, carry, h=h):
            for r in range(ROWS):
                i = g * ROWS + r
                out[h][rows(i, ly), :] = HALF[h, pl.ds(pl.multiple_of(i * pitch, ROWS), ly), :]
            return carry

        lax.fori_loop(0, lx // ROWS, planes, 0)

    Y.drain()


def sweep_scratch(count, most, tiles, parts):
    per, owners = split_tiles(tiles, most)
    return [
        pltpu.VMEM((tiles, 4, ROWS, LANES), jnp.float32),
        pltpu.VMEM((count, per, 4, ROWS, LANES), jnp.float32),
        pltpu.VMEM((tiles, 2, ROWS, LANES), jnp.float32),
        pltpu.VMEM((count, per, 2, ROWS, LANES), jnp.float32),
        pltpu.VMEM((count, per, 2, ROWS, LANES), jnp.float32),
        pltpu.VMEM((tiles, 2, ROWS, LANES), jnp.float32),
        pltpu.VMEM((count + 1, per, 2, ROWS, LANES), jnp.float32),
        pltpu.SemaphoreType.DMA((2, 2)),
        pltpu.SemaphoreType.DMA((1 + parts,)),
    ]


def gathered_scratch(count, tiles, parts):
    each = tiles // parts
    return [
        pltpu.VMEM((parts, each, 3, ROWS, LANES), jnp.float32),
        pltpu.VMEM((parts, count, each, 3, ROWS, LANES), jnp.float32),
        pltpu.VMEM((parts, each, 2, ROWS, LANES), jnp.float32),
        pltpu.VMEM((parts, count, each, ROWS, LANES), jnp.float32),
        pltpu.VMEM((parts, 2, each, ROWS, LANES), jnp.float32),
        pltpu.VMEM((parts, count + 1, 4, each, ROWS, LANES), jnp.float32),
        pltpu.SemaphoreType.DMA((2,)),
        pltpu.SemaphoreType.DMA((2 * parts,)),
    ]


def shards(nx, ny, field, cond_x, cond_y, cross_weight):
    lx, ly, nz = field.shape
    nh = nz // LANES
    cells = (nh, lx * ly, LANES)
    pitch = ly + ROWS if ly // ROWS % 2 == 0 else ly
    flat = [
        pltpu.with_memory_space_constraint(a.reshape(lx * ly, nz), pltpu.HBM)
        for a in (field, cond_x, cond_y, cross_weight)
    ]
    scratch = [
        pltpu.VMEM((nh, (lx + 2) * ly, LANES), jnp.float32),
        *[pltpu.VMEM(cells, jnp.float32)] * 4,
        pltpu.VMEM((nh, lx * pitch, LANES), jnp.float32),
        pltpu.VMEM(cells, jnp.float32),
        pltpu.VMEM((2, nh, ly, LANES), jnp.float32),
        pltpu.VMEM((2, nh, lx, LANES), jnp.float32),
        pltpu.VMEM((2, nh, lx, LANES), jnp.float32),
        pltpu.VMEM((4, nh, ROWS, LANES), jnp.float32),
        pltpu.VMEM((2, nh, lx, LANES), jnp.float32),
        pltpu.SemaphoreType.DMA((4, nh)),
        pltpu.SemaphoreType.DMA((8,)),
        pltpu.SemaphoreType.DMA((8,)),
        *sweep_scratch(nx, max(1, nx // 2), nh * ly // ROWS, nh),
        *gathered_scratch(ny, nh * lx // ROWS, nh),
    ]
    result = pl.pallas_call(
        functools.partial(kernel, nx, ny, lx, ly, nh, pitch),
        out_shape=[pltpu.VMEM((lx * ly, LANES), jnp.float32)] * nh,
        in_specs=[pl.BlockSpec(memory_space=pltpu.HBM)] * 4,
        out_specs=[pl.BlockSpec(memory_space=pltpu.VMEM)] * nh,
        scratch_shapes=scratch,
        compiler_params=pltpu.CompilerParams(
            collective_id=0, has_side_effects=True, vmem_limit_bytes=40 * 1024 * 1024
        ),
        cost_estimate=pl.CostEstimate(
            flops=60 * lx * ly * nz, bytes_accessed=20 * lx * ly * nz, transcendentals=0
        ),
        name="adi_step",
    )(*flat)
    return jnp.concatenate(result, axis=1).reshape(lx, ly, nz)


def solution(mesh):
    spec = P("gx", "gy", None)
    return jax.shard_map(
        functools.partial(shards, mesh.shape["gx"], mesh.shape["gy"]),
        mesh=mesh,
        in_specs=(spec,) * 4,
        out_specs=spec,
        check_vma=False,
    )
```
